128 devices in a mesh: wide: 8 (over z, core), group: 16 (over x, y).
Axes of the slice: x: 4, y: 4, z: 4, core: 2. Of those that a mesh axis runs over, the one named last changes fastest.
Arguments:
- residual: float32 [262144, 64], P(('wide', 'group')), may hold values from -6 to 6
- panels: float32 [256, 4, 1024], P(('wide', 'group')), may hold values from -1 to 1, as said below
- near_list: int32 [256, 16], P(('wide', 'group')), may hold values from 0 to 255, as said below
- near_len: int32 [256], P(('wide', 'group')), may hold values from 1 to 16
- far_list: int32 [256, 32], P(('wide', 'group')), may hold values from 0 to 255
- basis_far: float32 [256, 32, 1024], P(('wide', 'group')), may hold values from -0.1875 to 0.1875
- coupling: float32 [256, 32, 1024], P(('wide', 'group')), may hold values from -0.375 to 0.375
Outputs:
- basis_one: float32 [262144, 64], P(('wide', 'group'))
- basis_two: float32 [262144, 64], P(('wide', 'group'))
- factors: float32 [6, 64, 64], replicated
The draws below stay inside these ranges and needn't reach their ends.
Inputs may be any that keep to these rules, and one draw needn't show every extreme that they name: `near_list`: block i lies in group (i // 2) % 16. Entry 0 of row i is i; every other entry is a block of the same group as i. `panels`: coordinates in rows 0 to 2, weights in row 3 are positive.
All inputs are finite; a program needn't handle non-finite values.
Results may differ from the reference program's by a relative error of at most 0.0063.
Values may be sent and summed in bfloat16 or wider, within the bound.
A program may use at most 192 MiB of HBM per device.

```python
import jax
import jax.numpy as jnp
from jax import lax

B = 1024
R = 64
K = 32
BD = 2
NN = 16
NF = 32
WIDES = 8
GROUPS = 16
NB = 256
PANELS = 262144


def draw_panels(key, part):
    key = jax.random.fold_in(key, 11)
    key_pos, key_wt = jax.random.split(key)
    coords = jax.random.uniform(key_pos, (NB, 3, B), jnp.float32, -1.0, 1.0)
    weights = jnp.exp(jax.random.uniform(key_wt, (NB, 1, B), jnp.float32, jnp.log(0.005), jnp.log(0.05)))
    return jnp.concatenate([coords, weights], axis=1)


def draw_near_list(key, part):
    key = jax.random.fold_in(key, 12)
    key_w, key_b = jax.random.split(key)
    rows = jnp.arange(NB, dtype=jnp.int32)
    group_of = rows // BD % GROUPS
    pick_w = jax.random.randint(key_w, (NB, NN), 0, WIDES, jnp.int32)
    pick_b = jax.random.randint(key_b, (NB, NN), 0, BD, jnp.int32)
    ids = (pick_w * GROUPS + group_of[:, None]) * BD + pick_b
    return ids.at[:, 0].set(rows)


def draw_near_len(key, part):
    key = jax.random.fold_in(key, 13)
    counts = jax.random.randint(key, (NB,), 1, NN + 1, jnp.int32)
    return counts.at[0].set(NN)


def place_ends(result, stream_key, least, top_value):
    shape = result.shape
    place = [jax.random.randint(jax.random.fold_in(stream_key, axis), (), 0, shape[axis]) for axis in range(len(shape))]
    result = result.at[tuple(place)].set(least)
    longest = shape.index(max(shape))
    place[longest] = (place[longest] + 1) % shape[longest]
    return result.at[tuple(place)].set(top_value)


def steps_of(stream_key, shape, cuts, smallest, largest):
    def one(axis_at, blocks):
        draws = jax.random.uniform(jax.random.fold_in(jax.random.fold_in(stream_key, 6), axis_at), (blocks,), jnp.float32, smallest / len(cuts), largest / len(cuts))
        return jnp.repeat(jnp.exp(draws), shape[axis_at] // blocks).reshape((-1,) + (1,) * (len(shape) - axis_at - 1))

    loudness = one(*cuts[0])
    for cut in cuts[1:]:
        loudness = loudness * one(*cut)
    return loudness


def normal_values(key, shape, spread, limit, cuts=(), kind=jnp.bfloat16):
    factor_of = steps_of(key, shape, cuts, -0.22, 0.18) if cuts else 1.0
    array = jax.random.normal(key, shape, jnp.float32) * spread * factor_of
    return jnp.minimum(jnp.maximum(array, -limit), limit).astype(kind)


def setup_inputs(seed: int = 0) -> dict:
    splits = jax.random.split(jax.random.key(seed), 8)
    return {
        "residual": normal_values(splits[0], (PANELS, R), 1.0, 6.0, ((0, 128),), jnp.float32),
        "panels": draw_panels(jax.random.fold_in(splits[7], 71), 0),
        "near_list": draw_near_list(jax.random.fold_in(splits[7], 71), 0),
        "near_len": draw_near_len(jax.random.fold_in(splits[7], 71), 0),
        "far_list": place_ends(jax.random.randint(splits[4], (NB, NF), 0, NB), jax.random.fold_in(splits[4], 1), 0, NB - 1).astype(jnp.int32),
        "basis_far": normal_values(splits[5], (NB, K, B), B ** -0.5, 0.1875, ((0, 128),), jnp.float32),
        "coupling": normal_values(splits[6], (NB, K, NF * K), 0.06, 0.375, ((0, 128),), jnp.float32),
    }


HIGH = lax.Precision.HIGHEST

def near_kernel(own, other, weight_mask):
    dist_sq = jnp.zeros((own.shape[1], other.shape[1]), jnp.float32)
    for axis_c in range(3):
        gap = own[axis_c][:, None] - other[axis_c][None, :]
        dist_sq = dist_sq + gap * gap
    return ((other[3] * weight_mask)[None, :] * lax.rsqrt(dist_sq + 0.01)).astype(jnp.bfloat16)

def inner(left, right):
    return jnp.dot(left.T.astype(jnp.float32), right.astype(jnp.float32), precision=HIGH, preferred_element_type=jnp.float32) / PANELS

def orthonormal(block, lower):
    return lax.linalg.triangular_solve(lower, block, left_side=False, lower=True, transpose_a=True)

def reference(residual, panels, near_list, near_len, far_list, basis_far, coupling):
    slots = jnp.arange(NN)

    def apply(field):
        blocks = field.reshape(NB, B, R)
        rounded = blocks.astype(jnp.bfloat16)
        coeffs = jnp.einsum('jkq,jqr->jkr', basis_far, blocks, precision=HIGH)

        def row(index):
            ids = near_list[index]
            masks = (slots < near_len[index]).astype(jnp.float32)
            kernels = jax.vmap(near_kernel, (None, 0, 0))(panels[index], panels[ids], masks)
            near = jnp.einsum('npq,nqr->pr', kernels.astype(jnp.float32), rounded[ids].astype(jnp.float32), precision=HIGH)
            stacked = coeffs[far_list[index]].reshape(NF * K, R)
            inside = jnp.dot(coupling[index], stacked, precision=HIGH)
            far = jnp.dot(basis_far[index].T, inside, precision=HIGH)
            return 0.5 * blocks[index] + near + far
        return lax.map(row, jnp.arange(NB)).reshape(PANELS, R)
    chol0 = jnp.linalg.cholesky(inner(residual, residual))
    basis0 = orthonormal(residual, chol0)
    image1 = apply(basis0)
    h01 = inner(basis0, image1)
    new1 = image1 - jnp.dot(basis0, h01, precision=HIGH)
    chol1 = jnp.linalg.cholesky(inner(new1, new1))
    basis_one = orthonormal(new1, chol1)
    image2 = apply(basis_one)
    left = jnp.concatenate([basis0, basis_one], axis=1)
    heads = inner(left, image2)
    new2 = image2 - jnp.dot(left, heads, precision=HIGH)
    chol2 = jnp.linalg.cholesky(inner(new2, new2))
    basis_two = orthonormal(new2, chol2)
    factors = jnp.stack([chol0, h01, chol1, heads[:R], heads[R:], chol2])
    return (basis_one, basis_two, factors)
```

```python
import jax
import jax.numpy as jnp
from jax import lax
from jax.sharding import PartitionSpec as P

HIGH = lax.Precision.HIGHEST


def near_kernel(own, other, weight_mask):
    dist_sq = jnp.zeros((own.shape[1], other.shape[1]), jnp.float32)
    for axis_c in range(3):
        gap = own[axis_c][:, None] - other[axis_c][None, :]
        dist_sq = dist_sq + gap * gap
    return ((other[3] * weight_mask)[None, :] * lax.rsqrt(dist_sq + 0.01)).astype(jnp.bfloat16)


def project(left, right):
    return jnp.dot(left.T, right, precision=HIGH, preferred_element_type=jnp.float32)


def orthonormal(block, lower):
    return lax.linalg.triangular_solve(lower, block, left_side=False, lower=True, transpose_a=True)


def on_device(residual, panels, near_list, near_len, far_list, basis_far, coupling):
    groups = lax.axis_size("group")
    blocks_dev = panels.shape[0]
    width = panels.shape[2]
    rhs = residual.shape[1]
    slot_count = near_list.shape[1]
    total = float(lax.axis_size("wide") * groups * blocks_dev * width)
    group_panels = lax.all_gather(panels, "wide", axis=0, tiled=True)
    local_ids = near_list // blocks_dev // groups * blocks_dev + near_list % blocks_dev
    others = group_panels[local_ids].reshape(blocks_dev * slot_count, 4, width)
    owners = jnp.repeat(panels, slot_count, axis=0)
    masks = (jnp.arange(slot_count)[None, :] < near_len[:, None]).astype(jnp.float32).reshape(-1)
    near_blocks = lax.map(
        lambda item: near_kernel(item[0], item[1], item[2]), (owners, others, masks)
    )
    near_blocks = near_blocks.reshape(blocks_dev, slot_count, width, width)

    def apply(field):
        blocks = field.reshape(blocks_dev, width, rhs)
        high = blocks.astype(jnp.bfloat16)
        low = (blocks - high.astype(jnp.float32)).astype(jnp.bfloat16)
        parts = jnp.concatenate([high, low], axis=2)
        coeffs = jnp.einsum("bkq,bqr->bkr", basis_far, blocks, precision=HIGH).astype(jnp.bfloat16)
        every = lax.all_gather(coeffs, ("wide", "group"), axis=0, tiled=True)
        group_vectors = lax.all_gather(parts, "wide", axis=0, tiled=True)
        near_vectors = group_vectors[local_ids]
        near = jnp.einsum(
            "bnpq,bnqr->bpr", near_blocks, near_vectors, preferred_element_type=jnp.float32
        )
        near = near[:, :, :rhs] + near[:, :, rhs:]
        stacked = every[far_list].reshape(blocks_dev, -1, rhs).astype(jnp.float32)
        inside = jnp.einsum("bkm,bmr->bkr", coupling, stacked, precision=HIGH)
        far = jnp.einsum("bkp,bkr->bpr", basis_far, inside, precision=HIGH)
        return (near + far).reshape(blocks_dev * width, rhs)

    def lower_inverse(lower):
        return lax.linalg.triangular_solve(lower, jnp.eye(rhs, dtype=jnp.float32), left_side=True, lower=True)

    def dot(left, right):
        return jnp.dot(left, right, precision=HIGH)

    eye = jnp.eye(rhs, dtype=jnp.float32)
    image = apply(residual)
    pair = jnp.concatenate([residual, image], axis=1)
    gram = lax.psum(project(pair, pair), ("wide", "group")) / total
    image2 = apply(image)
    chol0 = jnp.linalg.cholesky(gram[:rhs, :rhs])
    inv0 = lower_inverse(chol0)
    h01 = dot(dot(inv0, gram[:rhs, rhs:]), inv0.T)
    chol1 = jnp.linalg.cholesky(dot(dot(inv0, gram[rhs:, rhs:]), inv0.T) - dot(h01.T, h01))
    inv1 = lower_inverse(chol1)
    basis0 = dot(residual, inv0.T)
    mix_new = dot(inv0.T, inv1.T)
    mix_old = dot(inv0.T, dot(h01, inv1.T))
    basis_one = dot(image, mix_new) - dot(residual, mix_old)
    second = dot(image2, mix_new) - dot(image, mix_old)
    left = jnp.concatenate([basis0, basis_one, second], axis=1)
    gram = lax.psum(project(left, second), ("wide", "group")) / total
    heads = gram[: 2 * rhs]
    chol2 = jnp.linalg.cholesky(gram[2 * rhs :] - dot(heads.T, heads))
    inv2 = lower_inverse(chol2)
    basis_two = dot(second - dot(left[:, : 2 * rhs], heads), inv2.T)
    factors = jnp.stack([chol0, h01 + 0.5 * eye, chol1, heads[:rhs], heads[rhs:] + 0.5 * eye, chol2])
    return (basis_one, basis_two, factors)


def solution(mesh):
    return jax.shard_map(
        on_device,
        mesh=mesh,
        in_specs=(
            P(("wide", "group"), None),
            P(("wide", "group"), None, None),
            P(("wide", "group"), None),
            P(("wide", "group")),
            P(("wide", "group"), None),
            P(("wide", "group"), None, None),
            P(("wide", "group"), None, None),
        ),
        out_specs=(P(("wide", "group"), None), P(("wide", "group"), None), P()),
        check_vma=False,
    )
```

```python
import jax
import jax.numpy as jnp
from jax import lax
from jax.experimental import pallas as pl
from jax.experimental.pallas import tpu as pltpu
from jax.sharding import PartitionSpec as P

HIGH = lax.Precision.HIGHEST
MESH = pl.DeviceIdType.MESH
F32 = jnp.float32
BF16 = jnp.bfloat16

B = 1024
R = 64
K = 32
NF = 32
DEPTH = 32
CHUNKS = 16
RESIDENT = 3
KEPT = 2 * RESIDENT
SMALL = 2.0 ** -30

NN_DIMS = (((1,), (0,)), ((), ()))
NT_DIMS = (((1,), (1,)), ((), ()))
TN_DIMS = (((0,), (0,)), ((), ()))


def exact(left, right, dims=NN_DIMS):
    return lax.dot_general(left, right, dims, precision=HIGH, preferred_element_type=F32)


def fast(left, right, dims=NN_DIMS):
    return lax.dot_general(left, right, dims, preferred_element_type=F32)


def two_parts(value):
    high = value.astype(BF16)
    return high, (value - high.astype(F32)).astype(BF16)


def three_parts(value):
    first = value.astype(BF16).astype(F32)
    rest = value - first
    second = rest.astype(BF16).astype(F32)
    return first, second, rest - second


class Place:
    def __init__(self):
        wide = lax.axis_index("wide")
        group = lax.axis_index("group")
        self.z, self.core = wide // 2, wide % 2
        self.x, self.y = group // 4, group % 4

    def wide(self, dz, flip):
        return (self.z + dz + 4) % 4 * 2 + (self.core + flip) % 2

    def device(self, dz=0, flip=0, dx=0, dy=0):
        return (self.wide(dz, flip), (self.x + dx + 4) % 4 * 4 + (self.y + dy + 4) % 4)


def remote(source, target, send, recv, device):
    return pltpu.make_async_remote_copy(
        src_ref=source, dst_ref=target, send_sem=send, recv_sem=recv, device_id=device, device_id_type=MESH
    )


class GroupGather:
    MOVES = (
        (0, 0, 2, 0, 1),
        (0, 0, 1, 1, 0),
        (0, 1, 1, 1, 0),
        (0, 1, 1, -1, 0),
        (0, 0, 1, -1, 0),
        (-1, 0, 1, 1, 0),
        (1, 1, 1, -1, 0),
        (-1, 0, 2, 0, 1),
        (1, 0, 2, 0, 1),
        (2, 0, 1, 0, 1),
        (2, 1, 1, 0, 1),
    )

    def __init__(self, place, buf, send, recv):
        self.place, self.buf, self.send, self.recv = place, buf, send, recv

    def copy(self, n):
        dz, first, count, to_z, flip = self.MOVES[n]
        part = self.buf.at[self.place.wide(dz, 0), pl.ds(first, count)]
        return remote(part, part, self.send.at[n], self.recv.at[n], self.place.device(to_z, flip))

    def start(self, *moves):
        for n in moves:
            self.copy(n).start()

    def wait(self, *moves):
        for n in moves:
            dz, first, count, to_z, flip = self.MOVES[n]
            part = self.buf.at[self.place.wide(dz - to_z, flip), pl.ds(first, count)]
            remote(part, part, self.send.at[n], self.recv.at[n], self.place.device(to_z, flip)).wait_recv()

    def finish(self):
        for n in range(len(self.MOVES)):
            self.copy(n).wait_send()


class CoefficientGather:
    def __init__(self, place, buf, send, recv):
        self.place, self.buf, self.send, self.recv = place, buf, send, recv

    def span(self, stage, back):
        here = self.place
        core, x, y, z = here.core, here.x, here.y, here.z
        if stage == 0:
            return ((core * 4 + x) * 4 + y) * 4 + (z - back + 4) % 4, 1
        if stage == 1:
            return ((core * 4 + x) * 4 + (y - back + 4) % 4) * 4, 4
        if stage == 2:
            return (core * 4 + (x - back + 4) % 4) * 16, 16
        return (core + back) % 2 * 64, 64

    def copy(self, stage, step, back):
        first, count = self.span(stage, back)
        part = self.buf.at[pl.ds(first, count)]
        target = (dict(dz=step), dict(dy=step), dict(dx=step), dict(flip=step))[stage]
        n = stage * 3 + step - 1
        return remote(part, part, self.send.at[n], self.recv.at[n], self.place.device(**target))

    def steps(self, stage):
        return (1,) if stage == 3 else (1, 2, 3)

    def start(self, stage):
        for step in self.steps(stage):
            self.copy(stage, step, 0).start()

    def wait(self, stage):
        for step in self.steps(stage):
            self.copy(stage, step, step).wait_recv()

    def finish(self):
        for stage in range(4):
            for step in self.steps(stage):
                self.copy(stage, step, 0).wait_send()


class AllReduce:
    def __init__(self, place, part, other, rings, full, send, recv):
        self.place, self.part, self.other, self.rings, self.full = place, part, other, rings, full
        self.send, self.recv = send, recv

    def swap(self):
        here = self.place
        return remote(
            self.part.at[1 - here.core], self.other, self.send.at[0], self.recv.at[0], here.device(flip=1)
        )

    def spot(self, stage):
        return (self.place.z, self.place.y, self.place.x)[stage]

    def copy(self, stage, step, back):
        slot = self.rings.at[stage, (self.spot(stage) - back + 4) % 4]
        target = (dict(dz=step), dict(dy=step), dict(dx=step))[stage]
        n = 1 + stage * 3 + step - 1
        return remote(slot, slot, self.send.at[n], self.recv.at[n], self.place.device(**target))

    def share(self, back):
        half = self.full.at[(self.place.core + back) % 2]
        return remote(half, half, self.send.at[10], self.recv.at[10], self.place.device(flip=1))

    def start(self):
        self.swap().start()

    def ring(self, stage):
        if stage == 0:
            self.swap().wait_recv()
            total = self.part[self.place.core] + self.other[...]
        else:
            for step in (1, 2, 3):
                self.copy(stage - 1, step, step).wait_recv()
            rings = self.rings
            total = (rings[stage - 1, 0] + rings[stage - 1, 1]) + (rings[stage - 1, 2] + rings[stage - 1, 3])
        if stage < 3:
            self.rings[stage, self.spot(stage)] = total
            for step in (1, 2, 3):
                self.copy(stage, step, 0).start()
        else:
            self.full[self.place.core] = total
            self.share(0).start()

    def wait(self):
        self.share(1).wait_recv()

    def finish(self):
        self.swap().wait_send()
        for stage in range(3):
            for step in (1, 2, 3):
                self.copy(stage, step, 0).wait_send()
        self.share(0).wait_send()


def cholesky(gram):
    lane = lax.broadcasted_iota(jnp.int32, (R, 2 * R), 1)
    row = lax.broadcasted_iota(jnp.int32, (R, 2 * R), 0)
    start = jnp.where(lane < R, jnp.where(lane == row, 1.0, 0.0), pltpu.roll(gram, R, 1))
    blocks = [start[8 * t : 8 * t + 8] for t in range(8)]
    rows = []
    for k in range(R):
        t, o = divmod(k, 8)
        line = blocks[t][o : o + 1]
        pivot = line[:, R + k : R + k + 1]
        root = lax.rsqrt(pivot)
        root = root * (1.5 - 0.5 * pivot * root * root)
        line = line * root
        rows.append(line)
        for u in range(t, 8):
            blocks[u] = blocks[u] - (blocks[u][:, R + k : R + k + 1] * root) * line
    done = jnp.concatenate(rows, axis=0)
    inverse = done[:, :R]
    upper = jnp.where(lane >= row, pltpu.roll(done, R, 1), 0.0)[:, :R]
    return inverse, upper


def step_kernel(
    res_ref, panels_ref, near_ref, len_ref, far_ref, basis_ref, coupling_ref,
    one_ref, two_ref, factors_ref, stored_ref,
    field, space, vectors, vectors2, coeffs, coeffs2, blocks, acc, counts, rows, own, coupled, stacked,
    part, other, rings, full, part2, other2, rings2, full2, left,
    near_send, near_recv, far_send, far_recv, sum_send, sum_recv, keep_sem, load_sem,
):
    here = Place()
    me = here.wide(0, 0)
    total = float(128 * 2 * B)

    barrier = pltpu.get_barrier_semaphore()
    partners = [here.device(flip=1)]
    for step in (1, 2, 3):
        partners += [here.device(dz=step), here.device(dy=step), here.device(dx=step)]
    for partner in partners:
        pl.semaphore_signal(barrier, inc=1, device_id=partner, device_id_type=MESH)

    for b in range(2):
        point = [panels_ref[b, a : a + 1, :] for a in range(3)]
        weight = jnp.maximum(panels_ref[b, 3:4, :], SMALL)
        scale = 1.0 / (weight * weight)
        square = point[0] * point[0] + point[1] * point[1] + point[2] * point[2]
        pairs = [(three_parts(-2.0 * point[a] * scale), three_parts(point[a])) for a in range(3)]
        pairs.append((three_parts(scale), three_parts(square)))
        line = 0
        for theirs, mine in pairs:
            for m, n in ((0, 0), (0, 1), (1, 0), (0, 2), (1, 1), (2, 0)):
                rows[0, line : line + 1, :] = theirs[m]
                rows[1, line : line + 1, :] = mine[n]
                line += 1
        for value in three_parts((square + 0.01) * scale):
            rows[0, line : line + 1, :] = value
            rows[1, line : line + 1, :] = jnp.ones((1, B), F32)
            line += 1
        rows[0, line:DEPTH, :] = jnp.zeros((DEPTH - line, B), F32)
        rows[1, line:DEPTH, :] = jnp.zeros((DEPTH - line, B), F32)
        space[me, b] = rows[0].astype(BF16)
        own[b] = rows[1].astype(BF16)

    def spread(source, target):
        for b in range(2):
            value = source[:, b * B : (b + 1) * B]
            weight = panels_ref[b, 3:4, :]
            high, low = two_parts(value * (weight / jnp.maximum(weight, SMALL)))
            target[me, b, :R] = high
            target[me, b, R:] = low

    def project(source, target):
        zero = jnp.zeros((R, B), F32)
        first = jnp.concatenate([source[:, :B], zero], axis=0)
        second = jnp.concatenate([zero, source[:, B:]], axis=0)
        value = exact(basis_ref[0], first, NT_DIMS) + exact(basis_ref[1], second, NT_DIMS)
        target[((here.core * 4 + here.x) * 4 + here.y) * 4 + here.z] = value.astype(BF16)

    near_space = GroupGather(here, space, near_send.at[0], near_recv.at[0])
    near_first = GroupGather(here, vectors, near_send.at[1], near_recv.at[1])
    near_second = GroupGather(here, vectors2, near_send.at[2], near_recv.at[2])
    far_first = CoefficientGather(here, coeffs, far_send.at[0], far_recv.at[0])
    far_second = CoefficientGather(here, coeffs2, far_send.at[1], far_recv.at[1])
    sum_first = AllReduce(here, part, other, rings, full, sum_send.at[0], sum_recv.at[0])
    sum_second = AllReduce(here, part2, other2, rings2, full2, sum_send.at[1], sum_recv.at[1])

    field[0:R, :] = res_ref[...]
    spread(field[0:R, :], vectors)
    pl.semaphore_wait(barrier, len(partners))
    near_space.start(0, 1, 3, 2, 4)
    near_first.start(0, 1, 3, 2, 4)
    project(field[0:R, :], coeffs)
    far_first.start(0)

    for i in range(2):
        ids = near_ref[i : i + 1, :]
        ids = (ids >> 5) * 2 + (ids & 1)
        wanted = lax.broadcasted_iota(jnp.int32, (16, 16), 0)
        slot = lax.broadcasted_iota(jnp.int32, (16, 16), 1)
        hit = jnp.where((ids == wanted) & (slot < len_ref[i]), 1.0, 0.0)
        counts[i] = jnp.broadcast_to(jnp.sum(hit, axis=1, keepdims=True), (16, 128))
        high, low = two_parts(coupling_ref[i])
        coupled[i, :K] = high
        coupled[i, K:] = low
        acc[i] = jnp.zeros((2 * R, B), F32)

    def source_of(c):
        s = c // 2

        def since(k):
            return (s + 8 - k) // 8

        flip = since(1) - since(2) + since(4) - since(6) + since(7)
        dz = since(2) + 2 * (since(3) - since(4)) + 2 * (since(5) - since(6)) + since(6)
        return here.wide(dz, flip)

    def slot_of(c):
        late = (c + CHUNKS - KEPT) // CHUNKS
        return c + late * (KEPT + c % 2 - c)

    def keep(c):
        return pltpu.make_async_copy(blocks.at[slot_of(c)], stored_ref.at[c - KEPT], keep_sem.at[c % 2])

    def load(c):
        return pltpu.make_async_copy(stored_ref.at[c - KEPT], blocks.at[slot_of(c)], load_sem.at[c % 2])

    def run(first, last, generate, values, events):
        def chunk(c, carry):
            for at, event in events.items():
                pl.when(c == at)(event)
            w, slot, i = source_of(c), slot_of(c), c % 2
            if generate:
                @pl.when(c >= KEPT + 2)
                def _():
                    keep(c - 2).wait()
            elif values is vectors2:
                @pl.when(c >= KEPT)
                def _():
                    load(c).wait()
            result = acc[i] if values is not None else None
            for b in range(2):
                if generate:
                    near = lax.rsqrt(fast(space[w, b], own[i], TN_DIMS)).astype(BF16)
                    blocks[slot, b] = near
                else:
                    near = blocks[slot, b]
                if values is not None:
                    times = counts[i, pl.ds(w * 2 + b, 1), :][:, :1]
                    result = result + times * fast(values[w, b], near)
            if values is not None:
                acc[i] = result
            if generate:
                @pl.when(c >= KEPT)
                def _():
                    keep(c).start()
            elif values is vectors2:
                @pl.when((c >= KEPT) & (c < CHUNKS - 2))
                def _():
                    load(c + 2).start()
            return carry

        lax.fori_loop(first, last, chunk, 0)

    def far_part(gathered, i):
        lane = lax.broadcasted_iota(jnp.int32, (K, 2 * R), 1)

        def entry(n, carry):
            block = far_ref[i, n]
            device, half = block >> 1, block & 1
            wide, group = device >> 4, device & 15
            slot = ((wide & 1) * 16 + group) * 4 + (wide >> 1)
            value = gathered[slot].astype(F32)
            stacked[pl.ds(pl.multiple_of(n * K, K), K), :] = jnp.where(lane // R == half, value, 0.0).astype(BF16)
            return carry

        lax.fori_loop(0, NF, entry, 0)
        inside = fast(coupled[i], stacked[...])
        inside = inside[:K] + inside[K:]
        result = exact(inside, basis_ref[i], TN_DIMS)
        return result[:R] + result[R:]

    def finish_rows(gathered, first):
        for i in range(2):
            near = acc[i]
            field[first : first + R, i * B : (i + 1) * B] = near[:R] + near[R:] + far_part(gathered, i)
            acc[i] = jnp.zeros((2 * R, B), F32)

    def before_2():
        near_space.wait(0)
        near_first.wait(0)
        near_space.wait(1, 3)
        near_space.start(5, 6)
        far_first.wait(0)
        far_first.start(1)

    run(0, 4, True, vectors, {2: before_2})

    def before_4():
        near_space.wait(2, 4)
        near_space.start(7, 8)

    def before_6():
        near_first.wait(1, 3)
        near_first.start(5, 6)
        far_first.wait(1)
        far_first.start(2)

    run(4, 8, True, None, {4: before_4, 6: before_6})
    near_first.wait(2, 4)
    near_first.start(7, 8)
    run(4, 8, False, vectors, {})

    def before_8():
        near_space.wait(5, 6)
        near_space.start(9, 10)
        near_space.wait(7, 8)
        near_first.wait(7, 8)

    def before_12():
        near_first.wait(5, 6)
        near_first.start(9, 10)
        near_space.wait(9, 10)
        far_first.wait(2)
        far_first.start(3)

    def before_14():
        near_first.wait(9, 10)

    run(8, 16, True, vectors, {8: before_8, 12: before_12, 14: before_14})
    far_first.wait(3)
    keep(CHUNKS - 2).wait()
    keep(CHUNKS - 1).wait()
    finish_rows(coeffs, R)

    spread(field[R : 2 * R, :], vectors2)
    near_second.start(0, 1, 3, 2, 4)
    load(KEPT).start()
    load(KEPT + 1).start()
    project(field[R : 2 * R, :], coeffs2)
    far_second.start(0)
    pair = field[0 : 2 * R, :]
    gram = exact(pair, pair, NT_DIMS) * (1.0 / total)
    part[0] = gram[:R]
    part[1] = gram[R:]
    sum_first.start()

    def second_2():
        sum_first.ring(0)
        far_second.wait(0)
        far_second.start(1)
        near_second.wait(0)

    run(0, 4, False, vectors2, {2: second_2})
    sum_first.ring(1)
    near_second.wait(1, 3)
    near_second.start(5, 6)
    sum_first.ring(2)
    far_second.wait(1)
    far_second.start(2)
    sum_first.ring(3)
    sum_first.wait()
    inverse0, upper0 = cholesky(full[0])
    cross = full[1][:, :R]
    square = pltpu.roll(full[1], R, 1)[:, :R]
    cross = exact(exact(inverse0, cross), inverse0, NT_DIMS)
    square = exact(exact(inverse0, square), inverse0, NT_DIMS) - exact(cross, cross, NT_DIMS)
    inverse1, upper1 = cholesky(jnp.concatenate([square, jnp.zeros((R, R), F32)], axis=1))
    mix_new = exact(inverse1, inverse0)
    mix_old = exact(exact(inverse1, cross), inverse0)
    eye = jnp.where(
        lax.broadcasted_iota(jnp.int32, (R, R), 0) == lax.broadcasted_iota(jnp.int32, (R, R), 1), 0.5, 0.0
    )
    factors_ref[0] = upper0
    factors_ref[1] = cross + eye
    factors_ref[2] = upper1
    left[0:R, :] = exact(inverse0, field[0:R, :])
    left[R : 2 * R, :] = exact(mix_new, field[R : 2 * R, :]) - exact(mix_old, field[0:R, :])
    one_ref[...] = left[R : 2 * R, :]

    def second_4():
        near_second.wait(2, 4)
        near_second.start(7, 8)

    def second_8():
        near_second.wait(5, 6)
        near_second.start(9, 10)
        near_second.wait(7, 8)
        far_second.wait(2)
        far_second.start(3)

    def second_14():
        near_second.wait(9, 10)

    run(4, 16, False, vectors2, {4: second_4, 8: second_8, 14: second_14})
    far_second.wait(3)
    finish_rows(coeffs2, 2 * R)

    left[2 * R :, :] = exact(mix_new, field[2 * R :, :]) - exact(mix_old, field[R : 2 * R, :])
    newest = left[2 * R :, :]
    part2[0] = exact(newest, left[0 : 2 * R, :], NT_DIMS) * (1.0 / total)
    part2[1] = jnp.concatenate([exact(newest, newest, NT_DIMS) * (1.0 / total), jnp.zeros((R, R), F32)], axis=1)
    sum_second.start()
    for stage in range(4):
        sum_second.ring(stage)
    sum_second.wait()
    heads = full2[0]
    rest = full2[1][:, :R] - exact(heads, heads, NT_DIMS)
    inverse2, upper2 = cholesky(jnp.concatenate([rest, jnp.zeros((R, R), F32)], axis=1))
    factors_ref[3] = heads[:, :R]
    factors_ref[4] = pltpu.roll(heads, R, 1)[:, :R] + eye
    factors_ref[5] = upper2
    two_ref[...] = exact(inverse2, newest - exact(heads, left[0 : 2 * R, :]))

    for gather in (near_space, near_first, near_second, far_first, far_second, sum_first, sum_second):
        gather.finish()


def on_device(residual, panels, near_list, near_len, far_list, basis_far, coupling):
    vmem = pl.BlockSpec(memory_space=pltpu.VMEM)
    smem = pl.BlockSpec(memory_space=pltpu.SMEM)
    wide = jax.ShapeDtypeStruct((R, 2 * B), F32)
    sums = [
        pltpu.VMEM((2, R, 2 * R), F32),
        pltpu.VMEM((R, 2 * R), F32),
        pltpu.VMEM((3, 4, R, 2 * R), F32),
        pltpu.VMEM((2, R, 2 * R), F32),
    ]
    one, two, factors, _ = pl.pallas_call(
        step_kernel,
        out_shape=(
            wide,
            wide,
            jax.ShapeDtypeStruct((6, R, R), F32),
            jax.ShapeDtypeStruct((CHUNKS - KEPT, 2, B, B), BF16),
        ),
        in_specs=[vmem, vmem, vmem, smem, smem, vmem, vmem],
        out_specs=(vmem, vmem, vmem, pl.BlockSpec(memory_space=pl.ANY)),
        scratch_shapes=[
            pltpu.VMEM((3 * R, 2 * B), F32),
            pltpu.VMEM((8, 2, DEPTH, B), BF16),
            pltpu.VMEM((8, 2, 2 * R, B), BF16),
            pltpu.VMEM((8, 2, 2 * R, B), BF16),
            pltpu.VMEM((128, K, 2 * R), BF16),
            pltpu.VMEM((128, K, 2 * R), BF16),
            pltpu.VMEM((KEPT + 2, 2, B, B), BF16),
            pltpu.VMEM((2, 2 * R, B), F32),
            pltpu.VMEM((2, 16, 128), F32),
            pltpu.VMEM((2, DEPTH, B), F32),
            pltpu.VMEM((2, DEPTH, B), BF16),
            pltpu.VMEM((2, 2 * K, NF * K), BF16),
            pltpu.VMEM((NF * K, 2 * R), BF16),
            *sums,
            *sums,
            pltpu.VMEM((3 * R, 2 * B), F32),
            pltpu.SemaphoreType.DMA((3, 11)),
            pltpu.SemaphoreType.DMA((3, 11)),
            pltpu.SemaphoreType.DMA((2, 10)),
            pltpu.SemaphoreType.DMA((2, 10)),
            pltpu.SemaphoreType.DMA((2, 11)),
            pltpu.SemaphoreType.DMA((2, 11)),
            pltpu.SemaphoreType.DMA((2,)),
            pltpu.SemaphoreType.DMA((2,)),
        ],
        compiler_params=pltpu.CompilerParams(
            collective_id=0, has_side_effects=True, vmem_limit_bytes=62 * 2**20
        ),
        cost_estimate=pl.CostEstimate(flops=17_000_000_000, bytes_accessed=80_000_000, transcendentals=33_554_432),
    )(residual.T, panels, near_list, near_len, far_list, basis_far, coupling)
    return (one.T, two.T, jnp.transpose(factors, (0, 2, 1)))


def solution(mesh):
    return jax.shard_map(
        on_device,
        mesh=mesh,
        in_specs=(
            P(("wide", "group"), None),
            P(("wide", "group"), None, None),
            P(("wide", "group"), None),
            P(("wide", "group")),
            P(("wide", "group"), None),
            P(("wide", "group"), None, None),
            P(("wide", "group"), None, None),
        ),
        out_specs=(P(("wide", "group"), None), P(("wide", "group"), None), P()),
        check_vma=False,
    )
```

```python
import jax
import jax.numpy as jnp
from jax import lax
from jax.experimental import pallas as pl
from jax.experimental.pallas import tpu as pltpu
from jax.sharding import PartitionSpec as P

HIGH = lax.Precision.HIGHEST
MESH = pl.DeviceIdType.MESH
F32 = jnp.float32
BF16 = jnp.bfloat16

B = 1024
R = 64
K = 32
NF = 32
DEPTH = 32
CHUNKS = 16
RESIDENT = 4
KEPT = 2 * RESIDENT
SMALL = 2.0 ** -30

NN_DIMS = (((1,), (0,)), ((), ()))
NT_DIMS = (((1,), (1,)), ((), ()))
TN_DIMS = (((0,), (0,)), ((), ()))


def exact(left, right, dims=NN_DIMS):
    return lax.dot_general(left, right, dims, precision=HIGH, preferred_element_type=F32)


def fast(left, right, dims=NN_DIMS):
    return lax.dot_general(left, right, dims, preferred_element_type=F32)


def two_parts(value):
    high = value.astype(BF16)
    return high, (value - high.astype(F32)).astype(BF16)


def close(left, right, dims=NN_DIMS):
    left_high, left_low = two_parts(left)
    right_high, right_low = two_parts(right)
    cross = fast(left_high, right_low, dims) + fast(left_low, right_high, dims)
    return fast(left_high, right_high, dims) + cross


def three_parts(value):
    first = value.astype(BF16).astype(F32)
    rest = value - first
    second = rest.astype(BF16).astype(F32)
    return first, second, rest - second


class Place:
    def __init__(self):
        wide = lax.axis_index("wide")
        group = lax.axis_index("group")
        self.z, self.core = wide // 2, wide % 2
        self.x, self.y = group // 4, group % 4

    def wide(self, dz, flip):
        return (self.z + dz + 4) % 4 * 2 + (self.core + flip) % 2

    def device(self, dz=0, flip=0, dx=0, dy=0):
        return (self.wide(dz, flip), (self.x + dx + 4) % 4 * 4 + (self.y + dy + 4) % 4)


def remote(source, target, send, recv, device):
    return pltpu.make_async_remote_copy(
        src_ref=source, dst_ref=target, send_sem=send, recv_sem=recv, device_id=device, device_id_type=MESH
    )


class GroupGather:
    MOVES = (
        (0, 0, 0, 1),
        (0, 1, 0, 1),
        (0, 0, 1, 0),
        (0, 1, 1, 0),
        (0, 1, -1, 0),
        (0, 0, -1, 0),
        (-1, 0, 1, 0),
        (1, 1, -1, 0),
        (-1, 0, 0, 1),
        (-1, 1, 0, 1),
        (1, 0, 0, 1),
        (1, 1, 0, 1),
        (2, 0, 0, 1),
        (2, 1, 0, 1),
    )

    def __init__(self, place, buf, send, recv):
        self.place, self.buf, self.send, self.recv = place, buf, send, recv

    def copy(self, n):
        dz, block, to_z, flip = self.MOVES[n]
        part = self.buf.at[self.place.wide(dz, 0), block]
        return remote(part, part, self.send.at[n], self.recv.at[n], self.place.device(to_z, flip))

    def start(self, *moves):
        for n in moves:
            self.copy(n).start()

    def wait(self, *moves):
        for n in moves:
            dz, block, to_z, flip = self.MOVES[n]
            part = self.buf.at[self.place.wide(dz - to_z, flip), block]
            remote(part, part, self.send.at[n], self.recv.at[n], self.place.device(to_z, flip)).wait_recv()

    def finish(self):
        for n in range(len(self.MOVES)):
            self.copy(n).wait_send()


class CoefficientGather:
    def __init__(self, place, buf, send, recv):
        self.place, self.buf, self.send, self.recv = place, buf, send, recv

    def span(self, stage, back):
        here = self.place
        core, x, y, z = here.core, here.x, here.y, here.z
        if stage == 0:
            return ((core * 4 + x) * 4 + y) * 4 + (z - back + 4) % 4, 1
        if stage == 1:
            return ((core * 4 + x) * 4 + (y - back + 4) % 4) * 4, 4
        if stage == 2:
            return (core * 4 + (x - back + 4) % 4) * 16, 16
        return (core + back) % 2 * 64, 64

    def copy(self, stage, step, back):
        first, count = self.span(stage, back)
        part = self.buf.at[pl.ds(first, count)]
        target = (dict(dz=step), dict(dy=step), dict(dx=step), dict(flip=step))[stage]
        n = stage * 3 + step - 1
        return remote(part, part, self.send.at[n], self.recv.at[n], self.place.device(**target))

    def steps(self, stage):
        return (1,) if stage == 3 else (1, 2, 3)

    def start(self, stage):
        for step in self.steps(stage):
            self.copy(stage, step, 0).start()

    def wait(self, stage):
        for step in self.steps(stage):
            self.copy(stage, step, step).wait_recv()

    def finish(self):
        for stage in range(4):
            for step in self.steps(stage):
                self.copy(stage, step, 0).wait_send()


class AllReduce:
    def __init__(self, place, part, other, rings, full, send, recv):
        self.place, self.part, self.other, self.rings, self.full = place, part, other, rings, full
        self.send, self.recv = send, recv

    def swap(self):
        here = self.place
        return remote(
            self.part.at[1 - here.core], self.other, self.send.at[0], self.recv.at[0], here.device(flip=1)
        )

    def spot(self, stage):
        return (self.place.z, self.place.y, self.place.x)[stage]

    def copy(self, stage, step, back):
        slot = self.rings.at[stage, (self.spot(stage) - back + 4) % 4]
        target = (dict(dz=step), dict(dy=step), dict(dx=step))[stage]
        n = 1 + stage * 3 + step - 1
        return remote(slot, slot, self.send.at[n], self.recv.at[n], self.place.device(**target))

    def share(self, back):
        half = self.full.at[(self.place.core + back) % 2]
        return remote(half, half, self.send.at[10], self.recv.at[10], self.place.device(flip=1))

    def start(self):
        self.swap().start()

    def ring(self, stage):
        if stage == 0:
            self.swap().wait_recv()
            total = self.part[self.place.core] + self.other[...]
        else:
            for step in (1, 2, 3):
                self.copy(stage - 1, step, step).wait_recv()
            rings = self.rings
            total = (rings[stage - 1, 0] + rings[stage - 1, 1]) + (rings[stage - 1, 2] + rings[stage - 1, 3])
        if stage < 3:
            self.rings[stage, self.spot(stage)] = total
            for step in (1, 2, 3):
                self.copy(stage, step, 0).start()
        else:
            self.full[self.place.core] = total
            self.share(0).start()

    def wait(self):
        self.share(1).wait_recv()

    def finish(self):
        self.swap().wait_send()
        for stage in range(3):
            for step in (1, 2, 3):
                self.copy(stage, step, 0).wait_send()
        self.share(0).wait_send()


def cholesky(gram):
    lane = lax.broadcasted_iota(jnp.int32, (R, 2 * R), 1)
    row = lax.broadcasted_iota(jnp.int32, (R, 2 * R), 0)
    start = jnp.where(lane < R, jnp.where(lane == row, 1.0, 0.0), pltpu.roll(gram, R, 1))
    blocks = [start[8 * t : 8 * t + 8] for t in range(8)]
    rows = []
    for t in range(8):
        cols = [
            {u: jnp.broadcast_to(blocks[u][:, R + k : R + k + 1], (8, 2 * R)) for u in range(t, 8)}
            for k in range(8 * t, 8 * t + 8)
        ]
        for j in range(8):
            root = lax.rsqrt(cols[j][t][j : j + 1])
            line = blocks[t][j : j + 1] * root
            rows.append(line)
            scaled = {u: cols[j][u] * root for u in range(t, 8)}
            for later in range(j + 1, 8):
                factor = scaled[t][later : later + 1]
                for u in range(t, 8):
                    cols[later][u] = cols[later][u] - scaled[u] * factor
            for u in range(t, 8):
                blocks[u] = blocks[u] - scaled[u] * line
    done = jnp.concatenate(rows, axis=0)
    inverse = done[:, :R]
    upper = jnp.where(lane >= row, pltpu.roll(done, R, 1), 0.0)[:, :R]
    return inverse, upper


def pack(wide, square):
    low = jnp.concatenate([square[: R // 2], square[R // 2 :]], axis=1)
    return jnp.concatenate([wide, low], axis=0).reshape(2, 48, 2 * R)


def unpack(value):
    value = value.reshape(96, 2 * R)
    low = value[R:]
    return value[:R], jnp.concatenate([low, pltpu.roll(low, R, 1)], axis=0)


def step_kernel(
    res_ref, panels_ref, near_ref, len_ref, far_ref, basis_ref, coupling_ref,
    left_ref, sums_ref, small_ref, stored_ref,
    field, space, vectors, vectors2, coeffs, coeffs2, blocks, acc, counts, rows, own, coupled, stacked,
    part, other, rings, full, part2, other2, rings2, full2, left,
    near_send, near_recv, far_send, far_recv, sum_send, sum_recv, keep_sem, load_sem, left_sem,
):
    here = Place()
    me = here.wide(0, 0)
    total = float(128 * 2 * B)

    barrier = pltpu.get_barrier_semaphore()
    partners = [here.device(flip=1)]
    for step in (1, 2, 3):
        partners += [here.device(dz=step), here.device(dy=step), here.device(dx=step)]
    for partner in partners:
        pl.semaphore_signal(barrier, inc=1, device_id=partner, device_id_type=MESH)

    for b in range(2):
        point = [panels_ref[b, a : a + 1, :] for a in range(3)]
        weight = jnp.maximum(panels_ref[b, 3:4, :], SMALL)
        scale = 1.0 / (weight * weight)
        square = point[0] * point[0] + point[1] * point[1] + point[2] * point[2]
        pairs = [(three_parts(-2.0 * point[a] * scale), three_parts(point[a])) for a in range(3)]
        pairs.append((three_parts(scale), three_parts(square)))
        line = 0
        for theirs, mine in pairs:
            for m, n in ((0, 0), (0, 1), (1, 0), (0, 2), (1, 1), (2, 0)):
                rows[0, line : line + 1, :] = theirs[m]
                rows[1, line : line + 1, :] = mine[n]
                line += 1
        for value in three_parts((square + 0.01) * scale):
            rows[0, line : line + 1, :] = value
            rows[1, line : line + 1, :] = jnp.ones((1, B), F32)
            line += 1
        rows[0, line:DEPTH, :] = jnp.zeros((DEPTH - line, B), F32)
        rows[1, line:DEPTH, :] = jnp.zeros((DEPTH - line, B), F32)
        space[me, b] = rows[0].astype(BF16)
        own[b] = rows[1].astype(BF16)

    def spread(source, target, b):
        weight = panels_ref[b, 3:4, :]
        target[me, b] = (source[:, b * B : (b + 1) * B] * (weight / jnp.maximum(weight, SMALL))).astype(BF16)

    def project(source, target):
        zero = jnp.zeros((R, B), F32)
        first = jnp.concatenate([source[:, :B], zero], axis=0)
        second = jnp.concatenate([zero, source[:, B:]], axis=0)
        value = close(basis_ref[0], first, NT_DIMS) + close(basis_ref[1], second, NT_DIMS)
        target[((here.core * 4 + here.x) * 4 + here.y) * 4 + here.z] = value.astype(BF16)

    near_space = GroupGather(here, space, near_send.at[0], near_recv.at[0])
    near_first = GroupGather(here, vectors, near_send.at[1], near_recv.at[1])
    near_second = GroupGather(here, vectors2, near_send.at[2], near_recv.at[2])
    far_first = CoefficientGather(here, coeffs, far_send.at[0], far_recv.at[0])
    far_second = CoefficientGather(here, coeffs2, far_send.at[1], far_recv.at[1])
    sum_first = AllReduce(here, part, other, rings, full, sum_send.at[0], sum_recv.at[0])
    sum_second = AllReduce(here, part2, other2, rings2, full2, sum_send.at[1], sum_recv.at[1])

    field[0:R, :] = res_ref[...]
    spread(res_ref, vectors, 0)
    spread(res_ref, vectors, 1)
    pl.semaphore_wait(barrier, len(partners))
    near_space.start(2, 4, 3, 5, 0, 1)
    near_first.start(2, 4, 3, 5, 0, 1)
    project(field[0:R, :], coeffs)
    far_first.start(0)

    for i in range(2):
        ids = near_ref[i : i + 1, :]
        ids = (ids >> 5) * 2 + (ids & 1)
        wanted = lax.broadcasted_iota(jnp.int32, (16, 16), 0)
        slot = lax.broadcasted_iota(jnp.int32, (16, 16), 1)
        hit = jnp.where((ids == wanted) & (slot < len_ref[i]), 1.0, 0.0)
        counts[i] = jnp.broadcast_to(jnp.sum(hit, axis=1, keepdims=True), (16, 128))
        high, low = two_parts(coupling_ref[i])
        coupled[i, :K] = high
        coupled[i, K:] = low
        acc[i] = jnp.zeros((R, B), F32)

    def row_of(c):
        late = c // 8
        return (1 - late) * (c % 2) + late * (c // 4 - 2)

    def source_of(c):
        late = c // 8
        s = (1 - late) * (c // 2) + late * (4 + c % 4)

        def since(k):
            return (s + 8 - k) // 8

        flip = since(1) - since(2) + since(4) - since(6) + since(7)
        dz = since(2) + 2 * (since(3) - since(4)) + 2 * (since(5) - since(6)) + since(6)
        return here.wide(dz, flip)

    def slot_of(c):
        late = (c + CHUNKS - KEPT) // CHUNKS
        return c + late * (KEPT + c % 2 - c)

    def keep(c):
        return pltpu.make_async_copy(blocks.at[slot_of(c)], stored_ref.at[c - KEPT], keep_sem.at[c % 2])

    def load(c):
        return pltpu.make_async_copy(stored_ref.at[c - KEPT], blocks.at[slot_of(c)], load_sem.at[c % 2])

    def run(first, last, generate, values, events):
        def chunk(c, carry):
            for at, event in events.items():
                pl.when(c == at)(event)
            w, slot, i = source_of(c), slot_of(c), row_of(c)
            if generate:
                @pl.when(c >= KEPT + 2)
                def _():
                    keep(c - 2).wait()
            elif values is vectors2:
                @pl.when(c >= KEPT)
                def _():
                    load(c).wait()
            result = acc[i] if values is not None else None
            for b in range(2):
                if generate:
                    near = lax.rsqrt(fast(space[w, b], own[i], TN_DIMS)).astype(BF16)
                    blocks[slot, b] = near
                else:
                    near = blocks[slot, b]
                if values is not None:
                    times = counts[i, pl.ds(w * 2 + b, 1), :][:, :1]
                    result = result + times * fast(values[w, b], near)
            if values is not None:
                acc[i] = result
            if generate:
                @pl.when(c >= KEPT)
                def _():
                    keep(c).start()
            elif values is vectors2:
                @pl.when((c >= KEPT) & (c < CHUNKS - 2))
                def _():
                    load(c + 2).start()
            return carry

        lax.fori_loop(first, last, chunk, 0)

    def far_part(gathered, i):
        lane = lax.broadcasted_iota(jnp.int32, (K, 2 * R), 1)

        def entry(n, carry):
            block = far_ref[i, n]
            device, half = block >> 1, block & 1
            wide, group = device >> 4, device & 15
            slot = ((wide & 1) * 16 + group) * 4 + (wide >> 1)
            value = gathered[slot].astype(F32)
            stacked[pl.ds(pl.multiple_of(n * K, K), K), :] = jnp.where(lane // R == half, value, 0.0).astype(BF16)
            return carry

        lax.fori_loop(0, NF, entry, 0, unroll=8)
        inside = fast(coupled[i], stacked[...])
        inside = inside[:K] + inside[K:]
        result = close(inside, basis_ref[i], TN_DIMS)
        return result[:R] + result[R:]

    def finish_row(gathered, first, i):
        field[first : first + R, i * B : (i + 1) * B] = acc[i] + far_part(gathered, i)
        acc[i] = jnp.zeros((R, B), F32)

    def before_2():
        near_space.wait(0, 1)
        near_first.wait(0, 1)

    def before_3():
        near_space.wait(2, 4)
        near_space.start(6, 7)
        far_first.wait(0)
        far_first.start(1)

    run(0, 4, True, vectors, {2: before_2, 3: before_3})

    def before_4():
        near_space.wait(3, 5)
        near_space.start(8, 9, 10, 11)

    def before_6():
        near_first.wait(2, 4)
        near_first.start(6, 7)
        far_first.wait(1)
        far_first.start(2)

    def before_7():
        near_space.wait(6, 7)
        near_space.start(12, 13)

    run(4, 8, True, None, {4: before_4, 6: before_6, 7: before_7})
    near_first.wait(3, 5)
    near_first.start(8, 9, 10, 11)
    run(4, 8, False, vectors, {})

    def before_8():
        near_space.wait(8, 9, 10, 11)
        near_first.wait(8, 9, 10, 11)
        near_first.wait(6, 7)
        near_first.start(12, 13)

    def before_10():
        near_space.wait(12, 13)
        far_first.wait(2)
        far_first.start(3)

    def before_11():
        near_first.wait(12, 13)

    def before_12():
        far_first.wait(3)
        finish_row(coeffs, R, 0)
        spread(field[R : 2 * R, :], vectors2, 0)
        near_second.start(2, 5, 0)

    def before_14():
        near_second.wait(2)
        near_second.start(6)

    def before_15():
        near_second.wait(5)
        near_second.start(8, 10)

    run(8, 16, True, vectors, {8: before_8, 10: before_10, 11: before_11, 12: before_12, 14: before_14, 15: before_15})
    finish_row(coeffs, R, 1)

    spread(field[R : 2 * R, :], vectors2, 1)
    near_second.start(4, 3, 1)
    keep(CHUNKS - 2).wait()
    load(KEPT).start()
    keep(CHUNKS - 1).wait()
    load(KEPT + 1).start()
    gram = close(field[R : 2 * R, :], field[0 : 2 * R, :], NT_DIMS) * (1.0 / total)
    first_gram = close(field[0:R, :], field[0:R, :], NT_DIMS) * (1.0 / total)
    part[...] = pack(gram, first_gram)
    sum_first.start()
    project(field[R : 2 * R, :], coeffs2)
    far_second.start(0)

    def second_2():
        sum_first.ring(0)
        near_second.wait(0, 1)

    def second_4():
        far_second.wait(0)
        far_second.start(1)
        near_second.wait(4)
        near_second.start(7)
        near_second.wait(3)
        near_second.start(9, 11)
        near_second.wait(6)
        near_second.start(12)
        sum_first.ring(1)

    def second_8():
        near_second.wait(8, 9, 10, 11)
        far_second.wait(1)
        far_second.start(2)

    def second_9():
        sum_first.ring(2)

    def second_10():
        near_second.wait(7)
        near_second.start(13)

    def second_11():
        near_second.wait(12, 13)

    def second_14():
        sum_first.ring(3)

    run(
        0, 16, False, vectors2,
        {2: second_2, 4: second_4, 8: second_8, 9: second_9, 10: second_10, 11: second_11, 14: second_14},
    )
    far_second.wait(2)
    far_second.start(3)
    sum_first.wait()
    gram, first_gram = unpack(full[...])
    inverse0, upper0 = cholesky(first_gram)
    cross = gram[:, :R]
    square = pltpu.roll(gram, R, 1)[:, :R]
    cross = exact(exact(inverse0, cross), inverse0, NT_DIMS)
    square = exact(exact(inverse0, square), inverse0, NT_DIMS) - exact(cross, cross, NT_DIMS)
    inverse1, upper1 = cholesky(jnp.concatenate([square, jnp.zeros((R, R), F32)], axis=1))
    mix_new = exact(inverse1, inverse0)
    mix_old = exact(exact(inverse1, cross), inverse0)
    small_ref[0] = upper0
    small_ref[1] = cross
    small_ref[2] = upper1
    left[0:R, :] = close(inverse0, field[0:R, :])
    mix = jnp.concatenate([-mix_old, mix_new], axis=1)
    left[R : 2 * R, :] = close(mix, field[0 : 2 * R, :])
    early = pltpu.make_async_copy(left.at[pl.ds(0, 2 * R)], left_ref.at[pl.ds(0, 2 * R)], left_sem.at[0])
    early.start()
    far_second.wait(3)
    finish_row(coeffs2, 2 * R, 0)
    finish_row(coeffs2, 2 * R, 1)

    left[2 * R :, :] = close(mix, field[R:, :])
    newest = left[2 * R :, :]
    late = pltpu.make_async_copy(left.at[pl.ds(2 * R, R)], left_ref.at[pl.ds(2 * R, R)], left_sem.at[1])
    late.start()
    heads = close(newest, left[0 : 2 * R, :], NT_DIMS) * (1.0 / total)
    part2[...] = pack(heads, close(newest, newest, NT_DIMS) * (1.0 / total))
    sum_second.start()
    for stage in range(4):
        sum_second.ring(stage)
    for gather in (near_space, near_first, near_second, far_first, far_second, sum_first):
        gather.finish()
    early.wait()
    late.wait()
    sum_second.wait()
    sums_ref[...] = full2[...]
    sum_second.finish()


def last_kernel(left_ref, sums_ref, small_ref, one_ref, two_ref, factors_ref):
    one_ref[...] = left_ref[R : 2 * R, :]
    heads, rest = unpack(sums_ref[...])
    rest = rest[:, :R] - exact(heads, heads, NT_DIMS)
    inverse, upper = cholesky(jnp.concatenate([rest, jnp.zeros((R, R), F32)], axis=1))
    mix = jnp.concatenate([-exact(inverse, heads[:, :R]), -exact(inverse, pltpu.roll(heads, R, 1)[:, :R])], axis=1)
    two_ref[...] = close(mix, left_ref[: 2 * R, :]) + close(inverse, left_ref[2 * R :, :])
    row = lax.broadcasted_iota(jnp.int32, (R, R), 0)
    lane = lax.broadcasted_iota(jnp.int32, (R, R), 1)
    half = jnp.where(row == lane, 0.5, 0.0)
    factors_ref[0] = small_ref[0].T
    factors_ref[1] = small_ref[1].T + half
    factors_ref[2] = small_ref[2].T
    factors_ref[3] = heads[:, :R].T
    factors_ref[4] = pltpu.roll(heads, R, 1)[:, :R].T + half
    factors_ref[5] = upper.T


def on_device(residual, panels, near_list, near_len, far_list, basis_far, coupling):
    vmem = pl.BlockSpec(memory_space=pltpu.VMEM)
    smem = pl.BlockSpec(memory_space=pltpu.SMEM)
    wide = jax.ShapeDtypeStruct((R, 2 * B), F32)
    sums = [
        pltpu.VMEM((2, 48, 2 * R), F32),
        pltpu.VMEM((48, 2 * R), F32),
        pltpu.VMEM((3, 4, 48, 2 * R), F32),
        pltpu.VMEM((2, 48, 2 * R), F32),
    ]
    left, sums_all, small, _ = pl.pallas_call(
        step_kernel,
        out_shape=(
            jax.ShapeDtypeStruct((3 * R, 2 * B), F32),
            jax.ShapeDtypeStruct((2, 48, 2 * R), F32),
            jax.ShapeDtypeStruct((3, R, R), F32),
            jax.ShapeDtypeStruct((CHUNKS - KEPT, 2, B, B), BF16),
        ),
        in_specs=[vmem, vmem, vmem, smem, smem, vmem, vmem],
        out_specs=(pl.BlockSpec(memory_space=pl.ANY), vmem, vmem, pl.BlockSpec(memory_space=pl.ANY)),
        scratch_shapes=[
            pltpu.VMEM((3 * R, 2 * B), F32),
            pltpu.VMEM((8, 2, DEPTH, B), BF16),
            pltpu.VMEM((8, 2, R, B), BF16),
            pltpu.VMEM((8, 2, R, B), BF16),
            pltpu.VMEM((128, K, 2 * R), BF16),
            pltpu.VMEM((128, K, 2 * R), BF16),
            pltpu.VMEM((KEPT + 2, 2, B, B), BF16),
            pltpu.VMEM((2, R, B), F32),
            pltpu.VMEM((2, 16, 128), F32),
            pltpu.VMEM((2, DEPTH, B), F32),
            pltpu.VMEM((2, DEPTH, B), BF16),
            pltpu.VMEM((2, 2 * K, NF * K), BF16),
            pltpu.VMEM((NF * K, 2 * R), BF16),
            *sums,
            *sums,
            pltpu.VMEM((3 * R, 2 * B), F32),
            pltpu.SemaphoreType.DMA((3, 14)),
            pltpu.SemaphoreType.DMA((3, 14)),
            pltpu.SemaphoreType.DMA((2, 10)),
            pltpu.SemaphoreType.DMA((2, 10)),
            pltpu.SemaphoreType.DMA((2, 11)),
            pltpu.SemaphoreType.DMA((2, 11)),
            pltpu.SemaphoreType.DMA((2,)),
            pltpu.SemaphoreType.DMA((2,)),
            pltpu.SemaphoreType.DMA((2,)),
        ],
        compiler_params=pltpu.CompilerParams(
            collective_id=0, has_side_effects=True, vmem_limit_bytes=62 * 2**20
        ),
        cost_estimate=pl.CostEstimate(flops=17_000_000_000, bytes_accessed=80_000_000, transcendentals=33_554_432),
    )(residual.T, panels, near_list, near_len, far_list, basis_far, coupling)
    one, two, factors = pl.pallas_call(
        last_kernel,
        out_shape=(wide, wide, jax.ShapeDtypeStruct((6, R, R), F32)),
        in_specs=[vmem, vmem, vmem],
        out_specs=(vmem, vmem, vmem),
        cost_estimate=pl.CostEstimate(flops=150_000_000, bytes_accessed=3_000_000, transcendentals=64),
    )(left, sums_all, small)
    return (one.T, two.T, factors)


def solution(mesh):
    return jax.shard_map(
        on_device,
        mesh=mesh,
        in_specs=(
            P(("wide", "group"), None),
            P(("wide", "group"), None, None),
            P(("wide", "group"), None),
            P(("wide", "group")),
            P(("wide", "group"), None),
            P(("wide", "group"), None, None),
            P(("wide", "group"), None, None),
        ),
        out_specs=(P(("wide", "group"), None), P(("wide", "group"), None), P()),
        check_vma=False,
    )
```

```python
import jax
import jax.numpy as jnp
from jax import lax
from jax.experimental import pallas as pl
from jax.experimental.pallas import tpu as pltpu
from jax.sharding import PartitionSpec as P

HIGH = lax.Precision.HIGHEST
MESH = pl.DeviceIdType.MESH
F32 = jnp.float32
BF16 = jnp.bfloat16

B = 1024
R = 64
K = 32
NF = 32
DEPTH = 32
PAIRS = 8
SMALL = 2.0 ** -30

NN_DIMS = (((1,), (0,)), ((), ()))
NT_DIMS = (((1,), (1,)), ((), ()))
TN_DIMS = (((0,), (0,)), ((), ()))


def exact(left, right, dims=NN_DIMS):
    return lax.dot_general(left, right, dims, precision=HIGH, preferred_element_type=F32)


def fast(left, right, dims=NN_DIMS):
    return lax.dot_general(left, right, dims, preferred_element_type=F32)


def two_parts(value):
    high = value.astype(BF16)
    return high, (value - high.astype(F32)).astype(BF16)


def close(left, right, dims=NN_DIMS):
    left_high, left_low = two_parts(left)
    right_high, right_low = two_parts(right)
    cross = fast(left_high, right_low, dims) + fast(left_low, right_high, dims)
    return fast(left_high, right_high, dims) + cross


def three_parts(value):
    first = value.astype(BF16).astype(F32)
    rest = value - first
    second = rest.astype(BF16).astype(F32)
    return first, second, rest - second


class Place:
    def __init__(self):
        wide = lax.axis_index("wide")
        group = lax.axis_index("group")
        self.z, self.core = wide // 2, wide % 2
        self.x, self.y = group // 4, group % 4

    def wide(self, dz, flip):
        return (self.z + dz + 4) % 4 * 2 + (self.core + flip) % 2

    def device(self, dz=0, flip=0, dx=0, dy=0):
        return (self.wide(dz, flip), (self.x + dx + 4) % 4 * 4 + (self.y + dy + 4) % 4)


def remote(source, target, send, recv, device):
    return pltpu.make_async_remote_copy(
        src_ref=source, dst_ref=target, send_sem=send, recv_sem=recv, device_id=device, device_id_type=MESH
    )


class GroupGather:
    MOVES = (
        (0, 0, 0, 1),
        (0, 1, 0, 1),
        (0, 0, 1, 0),
        (0, 1, 1, 0),
        (0, 1, -1, 0),
        (0, 0, -1, 0),
        (-1, 0, 1, 0),
        (1, 1, -1, 0),
        (-1, 0, 0, 1),
        (-1, 1, 0, 1),
        (1, 0, 0, 1),
        (1, 1, 0, 1),
        (2, 0, 0, 1),
        (2, 1, 0, 1),
    )

    def __init__(self, place, buf, send, recv):
        self.place, self.buf, self.send, self.recv = place, buf, send, recv

    def copy(self, n):
        dz, block, to_z, flip = self.MOVES[n]
        part = self.buf.at[self.place.wide(dz, 0), block]
        return remote(part, part, self.send.at[n], self.recv.at[n], self.place.device(to_z, flip))

    def start(self, *moves):
        for n in moves:
            self.copy(n).start()

    def wait(self, *moves):
        for n in moves:
            dz, block, to_z, flip = self.MOVES[n]
            part = self.buf.at[self.place.wide(dz - to_z, flip), block]
            remote(part, part, self.send.at[n], self.recv.at[n], self.place.device(to_z, flip)).wait_recv()

    def finish(self):
        for n in range(len(self.MOVES)):
            self.copy(n).wait_send()


class CoefficientGather:
    def __init__(self, place, buf, send, recv):
        self.place, self.buf, self.send, self.recv = place, buf, send, recv

    def axes(self, half):
        return (self.place.y, self.place.x) if half else (self.place.x, self.place.y)

    def slot(self, half):
        a, b = self.axes(half)
        return ((self.place.core * 4 + a) * 4 + b) * 4 + self.place.z

    def move(self, half, stage, step, back, flip=0):
        a, b = self.axes(half)
        core, z = (self.place.core + flip) % 2, self.place.z
        if stage == 0:
            first, count = ((core * 4 + a) * 4 + b) * 4 + (z - back + 4) % 4, 1
            target = dict(dz=step)
        elif stage == 1:
            first, count = ((core * 4 + a) * 4 + (b - back + 4) % 4) * 4, 4
            target = dict(dx=step) if half else dict(dy=step)
        elif stage == 2:
            first, count = (core * 4 + (a - back + 4) % 4) * 16, 16
            target = dict(dy=step) if half else dict(dx=step)
        else:
            first, count = (core * 4 + (a - step + 4) % 4) * 16, 16
            target = dict(flip=1)
        n = half * 13 + stage * 3 + (step if stage == 3 else step - 1)
        part = self.buf.at[half, pl.ds(first, count)]
        return remote(part, part, self.send.at[n], self.recv.at[n], self.place.device(**target))

    def start(self, stage):
        for half in range(2):
            for step in (1, 2, 3):
                self.move(half, stage, step, 0).start()
        if stage == 2:
            for half in range(2):
                self.move(half, 3, 0, 0).start()

    def wait(self, stage):
        for half in range(2):
            for step in (1, 2, 3):
                self.move(half, stage, step, step).wait_recv()

    def turn(self):
        for step in (1, 3, 2):
            for half in range(2):
                self.move(half, 2, step, step).wait_recv()
                self.move(half, 3, step, 0).start()

    def wait_other(self):
        for half in range(2):
            for step in range(4):
                self.move(half, 3, step, 0, 1).wait_recv()

    def finish(self):
        for half in range(2):
            for stage in range(3):
                for step in (1, 2, 3):
                    self.move(half, stage, step, 0).wait_send()
            for step in range(4):
                self.move(half, 3, step, 0).wait_send()


class AllReduce:
    def __init__(self, place, part, other, rings, full, send, recv):
        self.place, self.part, self.other, self.rings, self.full = place, part, other, rings, full
        self.send, self.recv = send, recv

    def swap(self):
        here = self.place
        return remote(
            self.part.at[1 - here.core], self.other, self.send.at[0], self.recv.at[0], here.device(flip=1)
        )

    def spot(self, stage):
        return (self.place.z, self.place.y, self.place.x)[stage]

    def copy(self, stage, step, back):
        slot = self.rings.at[stage, (self.spot(stage) - back + 4) % 4]
        target = (dict(dz=step), dict(dy=step), dict(dx=step))[stage]
        n = 1 + stage * 3 + step - 1
        return remote(slot, slot, self.send.at[n], self.recv.at[n], self.place.device(**target))

    def share(self, back):
        half = self.full.at[(self.place.core + back) % 2]
        return remote(half, half, self.send.at[10], self.recv.at[10], self.place.device(flip=1))

    def start(self):
        self.swap().start()

    def ring(self, stage):
        if stage == 0:
            self.swap().wait_recv()
            total = self.part[self.place.core] + self.other[...]
        else:
            for step in (1, 2, 3):
                self.copy(stage - 1, step, step).wait_recv()
            rings = self.rings
            total = (rings[stage - 1, 0] + rings[stage - 1, 1]) + (rings[stage - 1, 2] + rings[stage - 1, 3])
        if stage < 3:
            self.rings[stage, self.spot(stage)] = total
            for step in (1, 2, 3):
                self.copy(stage, step, 0).start()
        else:
            self.full[self.place.core] = total
            self.share(0).start()

    def wait(self):
        self.share(1).wait_recv()

    def finish(self):
        self.swap().wait_send()
        for stage in range(3):
            for step in (1, 2, 3):
                self.copy(stage, step, 0).wait_send()
        self.share(0).wait_send()


def cholesky(gram):
    lane = lax.broadcasted_iota(jnp.int32, (R, 2 * R), 1)
    row = lax.broadcasted_iota(jnp.int32, (R, 2 * R), 0)
    start = jnp.where(lane < R, jnp.where(lane == row, 1.0, 0.0), pltpu.roll(gram, R, 1))
    blocks = [start[8 * t : 8 * t + 8] for t in range(8)]
    rows = []
    for t in range(8):
        cols = [
            {u: jnp.broadcast_to(blocks[u][:, R + k : R + k + 1], (8, 2 * R)) for u in range(t, 8)}
            for k in range(8 * t, 8 * t + 8)
        ]
        for j in range(8):
            root = lax.rsqrt(cols[j][t][j : j + 1])
            line = blocks[t][j : j + 1] * root
            rows.append(line)
            scaled = {u: cols[j][u] * root for u in range(t, 8)}
            for later in range(j + 1, 8):
                factor = scaled[t][later : later + 1]
                for u in range(t, 8):
                    cols[later][u] = cols[later][u] - scaled[u] * factor
            for u in range(t, 8):
                blocks[u] = blocks[u] - scaled[u] * line
    done = jnp.concatenate(rows, axis=0)
    inverse = done[:, :R]
    upper = jnp.where(lane >= row, pltpu.roll(done, R, 1), 0.0)[:, :R]
    return inverse, upper


def pack(wide, square):
    low = jnp.concatenate([square[: R // 2], square[R // 2 :]], axis=1)
    return jnp.concatenate([wide, low], axis=0).reshape(2, 48, 2 * R)


def unpack(value):
    value = value.reshape(96, 2 * R)
    low = value[R:]
    return value[:R], jnp.concatenate([low, pltpu.roll(low, R, 1)], axis=0)


def step_kernel(
    res_ref, panels_ref, near_ref, len_ref, far_ref, basis_ref, coupling_ref,
    left_ref, sums_ref, small_ref, mixes_ref, stored_ref,
    field, space, vectors, vectors2, coeffs, coeffs2, blocks, acc, counts, rows, own, coupled, stacked,
    part, other, rings, full, part2, other2, rings2, full2, left,
    near_send, near_recv, far_send, far_recv, sum_send, sum_recv, keep_sem, load_sem, left_sem,
):
    here = Place()
    me = here.wide(0, 0)
    total = float(128 * 2 * B)

    barrier = pltpu.get_barrier_semaphore()
    partners = [here.device(flip=1)]
    for step in (1, 2, 3):
        partners += [here.device(dz=step), here.device(dy=step), here.device(dx=step)]
    for partner in partners:
        pl.semaphore_signal(barrier, inc=1, device_id=partner, device_id_type=MESH)

    for b in range(2):
        point = [panels_ref[b, a : a + 1, :] for a in range(3)]
        weight = jnp.maximum(panels_ref[b, 3:4, :], SMALL)
        scale = 1.0 / (weight * weight)
        square = point[0] * point[0] + point[1] * point[1] + point[2] * point[2]
        pairs = [(three_parts(-2.0 * point[a] * scale), three_parts(point[a])) for a in range(3)]
        pairs.append((three_parts(scale), three_parts(square)))
        line = 0
        for theirs, mine in pairs:
            for m, n in ((0, 0), (0, 1), (1, 0), (0, 2), (1, 1), (2, 0)):
                rows[0, line : line + 1, :] = theirs[m]
                rows[1, line : line + 1, :] = mine[n]
                line += 1
        for value in three_parts((square + 0.01) * scale):
            rows[0, line : line + 1, :] = value
            rows[1, line : line + 1, :] = jnp.ones((1, B), F32)
            line += 1
        rows[0, line:DEPTH, :] = jnp.zeros((DEPTH - line, B), F32)
        rows[1, line:DEPTH, :] = jnp.zeros((DEPTH - line, B), F32)
        space[me, b] = rows[0].astype(BF16)
        own[b] = rows[1].astype(BF16)

    def spread(source, target, b):
        weight = panels_ref[b, 3:4, :]
        target[me, b] = (source[:, b * B : (b + 1) * B] * (weight / jnp.maximum(weight, SMALL))).astype(BF16)

    def project(source, target):
        zero = jnp.zeros((R, B), F32)
        first = jnp.concatenate([source[:, :B], zero], axis=0)
        second = jnp.concatenate([zero, source[:, B:]], axis=0)
        value = close(basis_ref[0], first, NT_DIMS) + close(basis_ref[1], second, NT_DIMS)
        value = value.astype(BF16)
        target.buf[0, target.slot(0)] = value[: K // 2]
        target.buf[1, target.slot(1)] = value[K // 2 :]

    near_space = GroupGather(here, space, near_send.at[0], near_recv.at[0])
    near_first = GroupGather(here, vectors, near_send.at[1], near_recv.at[1])
    near_second = GroupGather(here, vectors2, near_send.at[2], near_recv.at[2])
    far_first = CoefficientGather(here, coeffs, far_send.at[0], far_recv.at[0])
    far_second = CoefficientGather(here, coeffs2, far_send.at[1], far_recv.at[1])
    sum_first = AllReduce(here, part, other, rings, full, sum_send.at[0], sum_recv.at[0])
    sum_second = AllReduce(here, part2, other2, rings2, full2, sum_send.at[1], sum_recv.at[1])

    field[0:R, :] = res_ref[...]
    spread(res_ref, vectors, 0)
    spread(res_ref, vectors, 1)
    project(field[0:R, :], far_first)
    pl.semaphore_wait(barrier, len(partners))
    near_space.start(2, 4, 3, 5, 0, 1)
    far_first.start(0)
    near_first.start(2, 4, 3, 5, 0, 1)

    for i in range(2):
        ids = near_ref[i : i + 1, :]
        ids = (ids >> 5) * 2 + (ids & 1)
        wanted = lax.broadcasted_iota(jnp.int32, (16, 16), 0)
        slot = lax.broadcasted_iota(jnp.int32, (16, 16), 1)
        hit = jnp.where((ids == wanted) & (slot < len_ref[i]), 1.0, 0.0)
        counts[i] = jnp.broadcast_to(jnp.sum(hit, axis=1, keepdims=True), (16, 128))
        high, low = two_parts(coupling_ref[i])
        coupled[i, :K] = high
        coupled[i, K:] = low
        acc[i] = jnp.zeros((R, B), F32)

    def row_of(c):
        late = c // 8
        return (1 - late) * (c % 2) + late * (c // 4 - 2)

    def source_of(c):
        late = c // 8
        s = (1 - late) * (c // 2) + late * (4 + c % 4)

        def since(k):
            return (s + 8 - k) // 8

        flip = since(1) - since(2) + since(4) - since(6) + since(7)
        dz = since(2) + 2 * (since(3) - since(4)) + 2 * (since(5) - since(6)) + since(6)
        return here.wide(dz, flip)

    def keep(t):
        return pltpu.make_async_copy(blocks.at[PAIRS + t % 2], stored_ref.at[t], keep_sem.at[t % 2])

    def load(t):
        return pltpu.make_async_copy(stored_ref.at[t], blocks.at[PAIRS + t % 2], load_sem.at[t % 2])

    def run(first, last, generate, values, events):
        def pair(t, carry):
            for at, event in events.items():
                pl.when(t == at)(event)
            if generate:
                @pl.when(t >= 2)
                def _():
                    keep(t - 2).wait()
            elif values is vectors2:
                load(t).wait()
            for c, slot in ((2 * t, PAIRS + t % 2), (2 * t + 1, t)):
                w, i = source_of(c), row_of(c)
                result = acc[i] if values is not None else None
                for b in range(2):
                    if generate:
                        near = lax.rsqrt(fast(space[w, b], own[i], TN_DIMS)).astype(BF16)
                        blocks[slot, b] = near
                    else:
                        near = blocks[slot, b]
                    if values is not None:
                        times = counts[i, pl.ds(w * 2 + b, 1), :][:, :1]
                        result = result + times * fast(values[w, b], near)
                if values is not None:
                    acc[i] = result
            if generate:
                keep(t).start()
            elif values is vectors2:
                @pl.when(t < PAIRS - 2)
                def _():
                    load(t + 2).start()
            return carry

        lax.fori_loop(first, last, pair, 0)

    def far_part(gathered, i):
        lane = lax.broadcasted_iota(jnp.int32, (K, 2 * R), 1)

        def entry(n, carry):
            block = far_ref[i, n]
            device, half = block >> 1, block & 1
            wide, group = device >> 4, device & 15
            core, z, x, y = wide & 1, wide >> 1, group >> 2, group & 3
            value = jnp.concatenate(
                [gathered[0, ((core * 4 + x) * 4 + y) * 4 + z], gathered[1, ((core * 4 + y) * 4 + x) * 4 + z]], axis=0
            ).astype(F32)
            stacked[pl.ds(pl.multiple_of(n * K, K), K), :] = jnp.where(lane // R == half, value, 0.0).astype(BF16)
            return carry

        lax.fori_loop(0, NF, entry, 0, unroll=8)
        inside = fast(coupled[i], stacked[...])
        inside = inside[:K] + inside[K:]
        result = close(inside, basis_ref[i], TN_DIMS)
        return result[:R] + result[R:]

    def finish_row(gathered, first, i):
        field[first : first + R, i * B : (i + 1) * B] = acc[i] + far_part(gathered, i)
        acc[i] = jnp.zeros((R, B), F32)

    def before_1():
        near_space.wait(0, 1)
        near_first.wait(0, 1)
        near_space.wait(2, 4)
        near_space.start(6, 7)
        far_first.wait(0)
        far_first.start(1)

    run(0, 2, True, vectors, {1: before_1})
    near_space.wait(3, 5)
    near_space.start(8, 9, 10, 11)
    run(2, 3, True, None, {})
    near_first.wait(2, 4)
    near_first.start(6, 7)
    near_first.wait(3, 5)
    near_first.start(8, 9, 10, 11)
    far_first.wait(1)
    far_first.start(2)
    run(2, 3, False, vectors, {})

    def before_4():
        near_space.wait(6, 7)
        near_space.start(12, 13)
        near_first.wait(6, 7)
        near_first.start(12, 13)
        near_space.wait(8, 9, 10, 11)
        near_first.wait(8, 9, 10, 11)

    def before_5():
        near_space.wait(12, 13)
        near_first.wait(12, 13)
        far_first.turn()

    def before_6():
        far_first.wait_other()
        finish_row(coeffs, R, 0)
        spread(field[R : 2 * R, :], vectors2, 0)
        near_second.start(2, 5, 0)

    def before_7():
        near_second.wait(2)
        near_second.start(6)
        near_second.wait(5)
        near_second.start(8, 10)

    run(3, 8, True, vectors, {4: before_4, 5: before_5, 6: before_6, 7: before_7})
    keep(PAIRS - 2).wait()
    load(0).start()
    finish_row(coeffs, R, 1)

    spread(field[R : 2 * R, :], vectors2, 1)
    project(field[R : 2 * R, :], far_second)
    far_second.start(0)
    near_second.start(4, 3, 1)
    keep(PAIRS - 1).wait()
    load(1).start()
    gram = close(field[R : 2 * R, :], field[0 : 2 * R, :], NT_DIMS) * (1.0 / total)
    part[...] = pack(gram, close(field[0:R, :], field[0:R, :], NT_DIMS) * (1.0 / total))
    sum_first.start()

    def second_1():
        near_second.wait(0, 1)
        sum_first.ring(0)
        far_second.wait(0)
        far_second.start(1)

    def second_2():
        near_second.wait(4)
        near_second.start(7)
        near_second.wait(3)
        near_second.start(9, 11)
        near_second.wait(6)
        near_second.start(12)

    def second_3():
        sum_first.ring(1)
        far_second.wait(1)
        far_second.start(2)

    def second_4():
        near_second.wait(7)
        near_second.start(13)
        near_second.wait(8, 9, 10, 11)

    def second_5():
        near_second.wait(12, 13)
        sum_first.ring(2)

    def second_7():
        far_second.turn()

    run(
        0, 8, False, vectors2,
        {1: second_1, 2: second_2, 3: second_3, 4: second_4, 5: second_5, 7: second_7},
    )
    sum_first.ring(3)
    far_second.wait_other()
    finish_row(coeffs2, 2 * R, 0)
    finish_row(coeffs2, 2 * R, 1)

    newest = field[2 * R :, :]
    cross = close(newest, field[0 : 2 * R, :], NT_DIMS) * (1.0 / total)
    part2[...] = pack(cross, close(newest, newest, NT_DIMS) * (1.0 / total))
    sum_second.start()
    sum_first.wait()
    gram, first_gram = unpack(full[...])
    sum_second.ring(0)
    inverse0, upper0 = cholesky(first_gram)
    square = pltpu.roll(gram, R, 1)[:, :R]
    cross = exact(exact(inverse0, gram[:, :R]), inverse0, NT_DIMS)
    square = exact(exact(inverse0, square), inverse0, NT_DIMS) - exact(cross, cross, NT_DIMS)
    small_ref[0] = upper0
    small_ref[1] = cross
    small_ref[3] = inverse0
    left[0:R, :] = close(inverse0, field[0:R, :])
    sum_second.ring(1)
    inverse1, upper1 = cholesky(jnp.concatenate([square, jnp.zeros((R, R), F32)], axis=1))
    small_ref[2] = upper1
    mix = jnp.concatenate([-exact(exact(inverse1, cross), inverse0), exact(inverse1, inverse0)], axis=1)
    mixes_ref[0] = gram
    mixes_ref[1] = mix
    left[R : 2 * R, :] = close(mix, field[0 : 2 * R, :])
    early = pltpu.make_async_copy(left.at[pl.ds(0, 2 * R)], left_ref.at[pl.ds(0, 2 * R)], left_sem.at[0])
    early.start()
    sum_second.ring(2)
    left[2 * R :, :] = close(mix, field[R:, :])
    late = pltpu.make_async_copy(left.at[pl.ds(2 * R, R)], left_ref.at[pl.ds(2 * R, R)], left_sem.at[1])
    late.start()
    for gather in (near_space, near_first, near_second, far_first, far_second, sum_first):
        gather.finish()
    early.wait()
    late.wait()
    sum_second.ring(3)
    sum_second.wait()
    sums_ref[...] = full2[...]
    sum_second.finish()


def last_kernel(left_hbm, sums_ref, small_ref, mixes_ref, one_ref, two_ref, factors_ref, left_ref, sem):
    fetch = pltpu.make_async_copy(left_hbm, left_ref, sem.at[0])
    fetch.start()
    hand_on = pltpu.make_async_copy(left_ref.at[pl.ds(R, R)], one_ref, sem.at[1])
    inverse0 = small_ref[3]
    gram, mix = mixes_ref[0], mixes_ref[1]
    cross, square = unpack(sums_ref[...])
    pair = exact(mix, jnp.concatenate([gram, cross], axis=0))
    heads0 = exact(pair[:, :R], inverse0, NT_DIMS)
    heads1 = exact(pair, mix, NT_DIMS)
    cross = pltpu.roll(cross, R, 1)[:, :R]
    square = jnp.concatenate(
        [
            jnp.concatenate([pltpu.roll(gram, R, 1)[:, :R], cross.T], axis=1),
            jnp.concatenate([cross, square[:, :R]], axis=1),
        ],
        axis=0,
    )
    rest = exact(exact(mix, square), mix, NT_DIMS) - exact(heads0, heads0, NT_DIMS) - exact(heads1, heads1, NT_DIMS)
    fetch.wait()
    hand_on.start()
    inverse, upper = cholesky(jnp.concatenate([rest, jnp.zeros((R, R), F32)], axis=1))
    last = jnp.concatenate([-exact(inverse, heads0), -exact(inverse, heads1)], axis=1)
    two_ref[...] = close(last, left_ref[: 2 * R, :]) + close(inverse, left_ref[2 * R :, :])
    row = lax.broadcasted_iota(jnp.int32, (R, R), 0)
    lane = lax.broadcasted_iota(jnp.int32, (R, R), 1)
    half = jnp.where(row == lane, 0.5, 0.0)
    factors_ref[0] = small_ref[0].T
    factors_ref[1] = small_ref[1].T + half
    factors_ref[2] = small_ref[2].T
    factors_ref[3] = heads0.T
    factors_ref[4] = heads1.T + half
    factors_ref[5] = upper.T
    hand_on.wait()


def on_device(residual, panels, near_list, near_len, far_list, basis_far, coupling):
    vmem = pl.BlockSpec(memory_space=pltpu.VMEM)
    smem = pl.BlockSpec(memory_space=pltpu.SMEM)
    wide = jax.ShapeDtypeStruct((R, 2 * B), F32)
    sums = [
        pltpu.VMEM((2, 48, 2 * R), F32),
        pltpu.VMEM((48, 2 * R), F32),
        pltpu.VMEM((3, 4, 48, 2 * R), F32),
        pltpu.VMEM((2, 48, 2 * R), F32),
    ]
    left, sums_all, small, mixes, _ = pl.pallas_call(
        step_kernel,
        out_shape=(
            jax.ShapeDtypeStruct((3 * R, 2 * B), F32),
            jax.ShapeDtypeStruct((2, 48, 2 * R), F32),
            jax.ShapeDtypeStruct((4, R, R), F32),
            jax.ShapeDtypeStruct((2, R, 2 * R), F32),
            jax.ShapeDtypeStruct((PAIRS, 2, B, B), BF16),
        ),
        in_specs=[vmem, vmem, vmem, smem, smem, vmem, vmem],
        out_specs=(pl.BlockSpec(memory_space=pl.ANY), vmem, vmem, vmem, pl.BlockSpec(memory_space=pl.ANY)),
        scratch_shapes=[
            pltpu.VMEM((3 * R, 2 * B), F32),
            pltpu.VMEM((8, 2, DEPTH, B), BF16),
            pltpu.VMEM((8, 2, R, B), BF16),
            pltpu.VMEM((8, 2, R, B), BF16),
            pltpu.VMEM((2, 128, K // 2, 2 * R), BF16),
            pltpu.VMEM((2, 128, K // 2, 2 * R), BF16),
            pltpu.VMEM((PAIRS + 2, 2, B, B), BF16),
            pltpu.VMEM((2, R, B), F32),
            pltpu.VMEM((2, 16, 128), F32),
            pltpu.VMEM((2, DEPTH, B), F32),
            pltpu.VMEM((2, DEPTH, B), BF16),
            pltpu.VMEM((2, 2 * K, NF * K), BF16),
            pltpu.VMEM((NF * K, 2 * R), BF16),
            *sums,
            *sums,
            pltpu.VMEM((3 * R, 2 * B), F32),
            pltpu.SemaphoreType.DMA((3, 14)),
            pltpu.SemaphoreType.DMA((3, 14)),
            pltpu.SemaphoreType.DMA((2, 26)),
            pltpu.SemaphoreType.DMA((2, 26)),
            pltpu.SemaphoreType.DMA((2, 11)),
            pltpu.SemaphoreType.DMA((2, 11)),
            pltpu.SemaphoreType.DMA((2,)),
            pltpu.SemaphoreType.DMA((2,)),
            pltpu.SemaphoreType.DMA((2,)),
        ],
        compiler_params=pltpu.CompilerParams(
            collective_id=0, has_side_effects=True, vmem_limit_bytes=62 * 2**20
        ),
        cost_estimate=pl.CostEstimate(flops=17_000_000_000, bytes_accessed=80_000_000, transcendentals=33_554_432),
    )(residual.T, panels, near_list, near_len, far_list, basis_far, coupling)
    one, two, factors = pl.pallas_call(
        last_kernel,
        out_shape=(wide, wide, jax.ShapeDtypeStruct((6, R, R), F32)),
        in_specs=[pl.BlockSpec(memory_space=pl.ANY), vmem, vmem, vmem],
        out_specs=(pl.BlockSpec(memory_space=pl.ANY), vmem, vmem),
        scratch_shapes=[pltpu.VMEM((3 * R, 2 * B), F32), pltpu.SemaphoreType.DMA((2,))],
        cost_estimate=pl.CostEstimate(flops=150_000_000, bytes_accessed=3_000_000, transcendentals=64),
    )(left, sums_all, small, mixes)
    return (one.T, two.T, factors)


def solution(mesh):
    return jax.shard_map(
        on_device,
        mesh=mesh,
        in_specs=(
            P(("wide", "group"), None),
            P(("wide", "group"), None, None),
            P(("wide", "group"), None),
            P(("wide", "group")),
            P(("wide", "group"), None),
            P(("wide", "group"), None, None),
            P(("wide", "group"), None, None),
        ),
        out_specs=(P(("wide", "group"), None), P(("wide", "group"), None), P()),
        check_vma=False,
    )
```

```python
import jax
import jax.numpy as jnp
from jax import lax
from jax.experimental import pallas as pl
from jax.experimental.pallas import tpu as pltpu
from jax.sharding import PartitionSpec as P

HIGH = lax.Precision.HIGHEST
MESH = pl.DeviceIdType.MESH
F32 = jnp.float32
BF16 = jnp.bfloat16

B = 1024
R = 64
K = 32
NF = 32
DEPTH = 32
PAIRS = 8
SMALL = 2.0 ** -30

NN_DIMS = (((1,), (0,)), ((), ()))
NT_DIMS = (((1,), (1,)), ((), ()))
TN_DIMS = (((0,), (0,)), ((), ()))


def exact(left, right, dims=NN_DIMS):
    return lax.dot_general(left, right, dims, precision=HIGH, preferred_element_type=F32)


def fast(left, right, dims=NN_DIMS):
    return lax.dot_general(left, right, dims, preferred_element_type=F32)


def two_parts(value):
    high = value.astype(BF16)
    return high, (value - high.astype(F32)).astype(BF16)


def close(left, right, dims=NN_DIMS):
    left_high, left_low = two_parts(left)
    right_high, right_low = two_parts(right)
    cross = fast(left_high, right_low, dims) + fast(left_low, right_high, dims)
    return fast(left_high, right_high, dims) + cross


def three_parts(value):
    first = value.astype(BF16).astype(F32)
    rest = value - first
    second = rest.astype(BF16).astype(F32)
    return first, second, rest - second


class Place:
    def __init__(self):
        wide = lax.axis_index("wide")
        group = lax.axis_index("group")
        self.z, self.core = wide // 2, wide % 2
        self.x, self.y = group // 4, group % 4

    def wide(self, dz, flip):
        return (self.z + dz + 4) % 4 * 2 + (self.core + flip) % 2

    def device(self, dz=0, flip=0, dx=0, dy=0):
        return (self.wide(dz, flip), (self.x + dx + 4) % 4 * 4 + (self.y + dy + 4) % 4)


def remote(source, target, send, recv, device):
    return pltpu.make_async_remote_copy(
        src_ref=source, dst_ref=target, send_sem=send, recv_sem=recv, device_id=device, device_id_type=MESH
    )


class GroupGather:
    MOVES = (
        (0, 0, 0, 1),
        (0, 1, 0, 1),
        (0, 0, 1, 0),
        (0, 1, 1, 0),
        (0, 1, -1, 0),
        (0, 0, -1, 0),
        (-1, 0, 1, 0),
        (1, 1, -1, 0),
        (-1, 0, 0, 1),
        (-1, 1, 0, 1),
        (1, 0, 0, 1),
        (1, 1, 0, 1),
        (2, 0, 0, 1),
        (2, 1, 0, 1),
    )

    def __init__(self, place, buf, send, recv):
        self.place, self.buf, self.send, self.recv = place, buf, send, recv

    def copy(self, n):
        dz, block, to_z, flip = self.MOVES[n]
        part = self.buf.at[self.place.wide(dz, 0), block]
        return remote(part, part, self.send.at[n], self.recv.at[n], self.place.device(to_z, flip))

    def start(self, *moves):
        for n in moves:
            self.copy(n).start()

    def wait(self, *moves):
        for n in moves:
            dz, block, to_z, flip = self.MOVES[n]
            part = self.buf.at[self.place.wide(dz - to_z, flip), block]
            remote(part, part, self.send.at[n], self.recv.at[n], self.place.device(to_z, flip)).wait_recv()

    def finish(self):
        for n in range(len(self.MOVES)):
            self.copy(n).wait_send()


class CoefficientGather:
    def __init__(self, place, buf, send, recv):
        self.place, self.buf, self.send, self.recv = place, buf, send, recv

    def axes(self, half):
        return (self.place.y, self.place.x) if half else (self.place.x, self.place.y)

    def slot(self, half):
        a, b = self.axes(half)
        return ((self.place.core * 4 + a) * 4 + b) * 4 + self.place.z

    def move(self, half, stage, step, back, flip=0):
        a, b = self.axes(half)
        core, z = (self.place.core + flip) % 2, self.place.z
        if stage == 0:
            first, count = ((core * 4 + a) * 4 + b) * 4 + (z - back + 4) % 4, 1
            target = dict(dz=step)
        elif stage == 1:
            first, count = ((core * 4 + a) * 4 + (b - back + 4) % 4) * 4, 4
            target = dict(dx=step) if half else dict(dy=step)
        elif stage == 2:
            first, count = (core * 4 + (a - back + 4) % 4) * 16, 16
            target = dict(dy=step) if half else dict(dx=step)
        else:
            first, count = (core * 4 + (a - step + 4) % 4) * 16, 16
            target = dict(flip=1)
        n = half * 13 + stage * 3 + (step if stage == 3 else step - 1)
        part = self.buf.at[half, pl.ds(first, count)]
        return remote(part, part, self.send.at[n], self.recv.at[n], self.place.device(**target))

    def start(self, stage):
        for half in range(2):
            for step in (1, 2, 3):
                self.move(half, stage, step, 0).start()
        if stage == 2:
            for half in range(2):
                self.move(half, 3, 0, 0).start()

    def wait(self, stage):
        for half in range(2):
            for step in (1, 2, 3):
                self.move(half, stage, step, step).wait_recv()

    def turn(self):
        for step in (1, 3, 2):
            for half in range(2):
                self.move(half, 2, step, step).wait_recv()
                self.move(half, 3, step, 0).start()

    def wait_other(self):
        for half in range(2):
            for step in range(4):
                self.move(half, 3, step, 0, 1).wait_recv()

    def finish(self):
        for half in range(2):
            for stage in range(3):
                for step in (1, 2, 3):
                    self.move(half, stage, step, 0).wait_send()
            for step in range(4):
                self.move(half, 3, step, 0).wait_send()


class AllReduce:
    PEERS = tuple((dz, flip) for dz in range(4) for flip in range(2) if dz + flip)

    def __init__(self, place, part, pieces, rings, full, send, recv):
        self.place, self.part, self.pieces, self.rings, self.full = place, part, pieces, rings, full
        self.send, self.recv = send, recv

    def scatter(self, n):
        here = self.place
        dz, flip = self.PEERS[n]
        return remote(
            self.part.at[here.wide(dz, flip)], self.pieces.at[here.wide(0, 0)],
            self.send.at[n], self.recv.at[n], here.device(dz, flip),
        )

    def copy(self, stage, step, back):
        here = self.place
        slot = self.rings.at[stage, ((here.y, here.x)[stage] - back + 4) % 4]
        target = (dict(dy=step), dict(dx=step))[stage]
        n = 7 + stage * 3 + step - 1
        return remote(slot, slot, self.send.at[n], self.recv.at[n], here.device(**target))

    def share(self, n):
        here = self.place
        dz, flip = self.PEERS[n]
        piece = self.full.at[here.wide(0, 0)]
        return remote(piece, piece, self.send.at[13 + n], self.recv.at[13 + n], here.device(dz, flip))

    def arrival(self, buffer, n, sem):
        here = self.place
        dz, flip = self.PEERS[n]
        piece = buffer.at[here.wide(-dz, flip)]
        return remote(piece, piece, self.send.at[sem], self.recv.at[sem], here.device(dz, flip))

    def start(self):
        for n in range(7):
            self.scatter(n).start()

    def ring(self, stage):
        here = self.place
        if stage == 0:
            for n in range(7):
                self.arrival(self.pieces, n, n).wait_recv()
            p = self.pieces
            me = here.wide(0, 0)
            p[me] = self.part[me]
            total = ((p[0] + p[1]) + (p[2] + p[3])) + ((p[4] + p[5]) + (p[6] + p[7]))
        else:
            for step in (1, 2, 3):
                self.copy(stage - 1, step, step).wait_recv()
            rings = self.rings
            total = (rings[stage - 1, 0] + rings[stage - 1, 1]) + (rings[stage - 1, 2] + rings[stage - 1, 3])
        if stage < 2:
            self.rings[stage, (here.y, here.x)[stage]] = total
            for step in (1, 2, 3):
                self.copy(stage, step, 0).start()
        else:
            self.full[here.wide(0, 0)] = total
            for n in range(7):
                self.share(n).start()

    def wait(self):
        for n in range(7):
            self.arrival(self.full, n, 13 + n).wait_recv()

    def finish(self):
        for n in range(7):
            self.scatter(n).wait_send()
            self.share(n).wait_send()
        for stage in range(2):
            for step in (1, 2, 3):
                self.copy(stage, step, 0).wait_send()


def cholesky(gram):
    lane = lax.broadcasted_iota(jnp.int32, (R, 2 * R), 1)
    row = lax.broadcasted_iota(jnp.int32, (R, 2 * R), 0)
    start = jnp.where(lane < R, jnp.where(lane == row, 1.0, 0.0), pltpu.roll(gram, R, 1))
    blocks = [start[8 * t : 8 * t + 8] for t in range(8)]
    rows = []
    for t in range(8):
        cols = [
            {u: jnp.broadcast_to(blocks[u][:, R + k : R + k + 1], (8, 2 * R)) for u in range(t, 8)}
            for k in range(8 * t, 8 * t + 8)
        ]
        for j in range(8):
            root = lax.rsqrt(cols[j][t][j : j + 1])
            line = blocks[t][j : j + 1] * root
            rows.append(line)
            scaled = {u: cols[j][u] * root for u in range(t, 8)}
            for later in range(j + 1, 8):
                factor = scaled[t][later : later + 1]
                for u in range(t, 8):
                    cols[later][u] = cols[later][u] - scaled[u] * factor
            for u in range(t, 8):
                blocks[u] = blocks[u] - scaled[u] * line
    done = jnp.concatenate(rows, axis=0)
    inverse = done[:, :R]
    upper = jnp.where(lane >= row, pltpu.roll(done, R, 1), 0.0)[:, :R]
    return inverse, upper


def pack(wide, square):
    return jnp.concatenate([wide, jnp.concatenate([square, square], axis=1)], axis=0).reshape(8, 16, 2 * R)


def unpack(value):
    value = value.reshape(2 * R, 2 * R)
    return value[:R], value[R:]


def step_kernel(
    res_hbm, panels_hbm, near_ref, len_ref, far_ref, far_vec_ref, basis_hbm, coupling_hbm,
    left_ref, sums_ref, small_ref, mixes_ref, stored_ref,
    field, space, vectors, vectors2, coeffs, coeffs2, blocks, acc, counts, rows, own, coupled, stacked,
    part, other, rings, full, part2, other2, rings2, full2, left,
    near_send, near_recv, far_send, far_recv, sum_send, sum_recv, keep_sem, load_sem, left_sem,
    res_ref, panels_ref, basis_ref, coupling_ref, input_sem,
):
    here = Place()
    me = here.wide(0, 0)
    total = float(128 * 2 * B)

    barrier = pltpu.get_barrier_semaphore()
    partners = [here.device(flip=1)]
    for step in (1, 2, 3):
        partners += [here.device(dz=step), here.device(dz=step, flip=1), here.device(dy=step), here.device(dx=step)]
    for partner in partners:
        pl.semaphore_signal(barrier, inc=1, device_id=partner, device_id_type=MESH)

    inputs = [
        pltpu.make_async_copy(source, target, input_sem.at[n])
        for n, (source, target) in enumerate(
            ((panels_hbm, panels_ref), (res_hbm, res_ref), (basis_hbm, basis_ref), (coupling_hbm, coupling_ref))
        )
    ]
    for copy in inputs:
        copy.start()
    inputs[0].wait()

    for b in range(2):
        point = [panels_ref[b, a : a + 1, :] for a in range(3)]
        weight = jnp.maximum(panels_ref[b, 3:4, :], SMALL)
        scale = 1.0 / (weight * weight)
        square = point[0] * point[0] + point[1] * point[1] + point[2] * point[2]
        pairs = [(three_parts(-2.0 * point[a] * scale), three_parts(point[a])) for a in range(3)]
        pairs.append((three_parts(scale), three_parts(square)))
        line = 0
        for theirs, mine in pairs:
            for m, n in ((0, 0), (0, 1), (1, 0), (0, 2), (1, 1), (2, 0)):
                rows[0, line : line + 1, :] = theirs[m]
                rows[1, line : line + 1, :] = mine[n]
                line += 1
        for value in three_parts((square + 0.01) * scale):
            rows[0, line : line + 1, :] = value
            rows[1, line : line + 1, :] = jnp.ones((1, B), F32)
            line += 1
        rows[0, line:DEPTH, :] = jnp.zeros((DEPTH - line, B), F32)
        rows[1, line:DEPTH, :] = jnp.zeros((DEPTH - line, B), F32)
        space[me, b] = rows[0].astype(BF16)
        own[b] = rows[1].astype(BF16)

    def spread(source, target, b):
        weight = panels_ref[b, 3:4, :]
        target[me, b] = (source[:, b * B : (b + 1) * B] * (weight / jnp.maximum(weight, SMALL))).astype(BF16)

    def project(source, target):
        zero = jnp.zeros((R, B), F32)
        first = jnp.concatenate([source[:, :B], zero], axis=0)
        second = jnp.concatenate([zero, source[:, B:]], axis=0)
        value = close(basis_ref[0], first, NT_DIMS) + close(basis_ref[1], second, NT_DIMS)
        value = value.astype(BF16)
        target.buf[0, target.slot(0)] = value[: K // 2]
        target.buf[1, target.slot(1)] = value[K // 2 :]

    near_space = GroupGather(here, space, near_send.at[0], near_recv.at[0])
    near_first = GroupGather(here, vectors, near_send.at[1], near_recv.at[1])
    near_second = GroupGather(here, vectors2, near_send.at[2], near_recv.at[2])
    far_first = CoefficientGather(here, coeffs, far_send.at[0], far_recv.at[0])
    far_second = CoefficientGather(here, coeffs2, far_send.at[1], far_recv.at[1])
    sum_first = AllReduce(here, part, other, rings, full, sum_send.at[0], sum_recv.at[0])
    sum_second = AllReduce(here, part2, other2, rings2, full2, sum_send.at[1], sum_recv.at[1])

    inputs[1].wait()
    field[0:R, :] = res_ref[...]
    spread(res_ref, vectors, 0)
    spread(res_ref, vectors, 1)
    inputs[2].wait()
    project(field[0:R, :], far_first)
    inputs[3].wait()
    for i in range(2):
        ids = near_ref[i : i + 1, :]
        ids = (ids >> 5) * 2 + (ids & 1)
        wanted = lax.broadcasted_iota(jnp.int32, (16, 16), 0)
        slot = lax.broadcasted_iota(jnp.int32, (16, 16), 1)
        hit = jnp.where((ids == wanted) & (slot < len_ref[i]), 1.0, 0.0)
        counts[i] = jnp.broadcast_to(jnp.sum(hit, axis=1, keepdims=True), (16, 128))
        odd = jnp.broadcast_to(far_vec_ref[i : i + 1, :] & 1, (8, NF)).astype(F32)
        spot = lax.broadcasted_iota(jnp.int32, (NF, NF * K), 1) // K
        entry = lax.broadcasted_iota(jnp.int32, (NF, NF * K), 0)
        odd = fast(odd.astype(BF16), jnp.where(spot == entry, 1.0, 0.0).astype(BF16))[0:1]
        for at, keep_it in ((0, 1.0 - odd), (2 * K, odd)):
            high, low = two_parts(coupling_ref[i] * keep_it)
            coupled[i, at : at + K] = high
            coupled[i, at + K : at + 2 * K] = low
        acc[i] = jnp.zeros((R, B), F32)

    pl.semaphore_wait(barrier, len(partners))
    near_space.start(2, 4, 3, 5, 0, 1)
    far_first.start(0)
    near_first.start(2, 4, 3, 5, 0, 1)

    def row_of(c):
        late = c // 8
        return (1 - late) * (c % 2) + late * (c // 4 - 2)

    def source_of(c):
        late = c // 8
        s = (1 - late) * (c // 2) + late * (4 + c % 4)

        def since(k):
            return (s + 8 - k) // 8

        flip = since(1) - since(2) + since(4) - since(6) + since(7)
        dz = since(2) + 2 * (since(3) - since(4)) + 2 * (since(5) - since(6)) + since(6)
        return here.wide(dz, flip)

    def keep(t):
        return pltpu.make_async_copy(blocks.at[PAIRS + t % 2], stored_ref.at[t], keep_sem.at[t % 2])

    def load(t):
        return pltpu.make_async_copy(stored_ref.at[t], blocks.at[PAIRS + t % 2], load_sem.at[t % 2])

    def run(first, last, generate, values, events):
        def pair(t, carry):
            for at, event in events.items():
                pl.when(t == at)(event)
            if generate:
                @pl.when(t >= 2)
                def _():
                    keep(t - 2).wait()
            elif values is vectors2:
                load(t).wait()
            for c, slot in ((2 * t, PAIRS + t % 2), (2 * t + 1, t)):
                w, i = source_of(c), row_of(c)
                result = acc[i] if values is not None else None
                for b in range(2):
                    if generate:
                        near = lax.rsqrt(fast(space[w, b], own[i], TN_DIMS)).astype(BF16)
                        blocks[slot, b] = near
                    else:
                        near = blocks[slot, b]
                    if values is not None:
                        times = counts[i, pl.ds(w * 2 + b, 1), :][:, :1]
                        result = result + times * fast(values[w, b], near)
                if values is not None:
                    acc[i] = result
            if generate:
                keep(t).start()
            elif values is vectors2:
                @pl.when(t < PAIRS - 2)
                def _():
                    load(t + 2).start()
            return carry

        lax.fori_loop(first, last, pair, 0)

    def far_part(gathered, i):
        def entry(n, carry):
            device = far_ref[i, n] >> 1
            wide, group = device >> 4, device & 15
            core, z, x, y = wide & 1, wide >> 1, group >> 2, group & 3
            stacked[pl.ds(pl.multiple_of(n * K, K), K // 2), :] = gathered[0, ((core * 4 + x) * 4 + y) * 4 + z]
            stacked[pl.ds(pl.multiple_of(n * K + K // 2, K // 2), K // 2), :] = gathered[
                1, ((core * 4 + y) * 4 + x) * 4 + z
            ]
            return carry

        lax.fori_loop(0, NF, entry, 0, unroll=8)
        inside = fast(coupled[i], stacked[...])
        first = lax.broadcasted_iota(jnp.int32, (K, 2 * R), 1) < R
        inside = jnp.where(first, inside[:K] + inside[K : 2 * K], inside[2 * K : 3 * K] + inside[3 * K :])
        result = close(inside, basis_ref[i], TN_DIMS)
        return result[:R] + result[R:]

    def finish_row(gathered, first, i):
        field[first : first + R, i * B : (i + 1) * B] = acc[i] + far_part(gathered, i)
        acc[i] = jnp.zeros((R, B), F32)

    def before_1():
        near_space.wait(0, 1)
        near_first.wait(0, 1)
        near_space.wait(2, 4)
        near_space.start(6, 7)

    run(0, 2, True, vectors, {1: before_1})
    near_space.wait(3, 5)
    near_space.start(8, 9, 10, 11)
    far_first.wait(0)
    far_first.start(1)
    run(2, 3, True, None, {})
    near_first.wait(2, 4)
    near_first.start(6, 7)
    near_first.wait(3, 5)
    near_first.start(8, 9, 10, 11)
    run(2, 3, False, vectors, {})
    far_first.wait(1)
    far_first.start(2)

    def before_4():
        near_space.wait(6, 7)
        near_space.start(12, 13)
        near_first.wait(6, 7)
        near_first.start(12, 13)
        near_space.wait(8, 9, 10, 11)
        near_first.wait(8, 9, 10, 11)

    def before_5():
        near_space.wait(12, 13)
        near_first.wait(12, 13)
        far_first.turn()

    def before_6():
        far_first.wait_other()
        finish_row(coeffs, R, 0)
        spread(field[R : 2 * R, :], vectors2, 0)
        near_second.start(2, 5, 0)

    def before_7():
        near_second.wait(2)
        near_second.start(6)
        near_second.wait(5)
        near_second.start(8, 10)

    run(3, 8, True, vectors, {4: before_4, 5: before_5, 6: before_6, 7: before_7})
    keep(PAIRS - 2).wait()
    load(0).start()
    finish_row(coeffs, R, 1)

    spread(field[R : 2 * R, :], vectors2, 1)
    project(field[R : 2 * R, :], far_second)
    far_second.start(0)
    near_second.start(4, 3, 1)
    keep(PAIRS - 1).wait()
    load(1).start()
    gram = close(field[R : 2 * R, :], field[0 : 2 * R, :], NT_DIMS) * (1.0 / total)
    part[...] = pack(gram, close(field[0:R, :], field[0:R, :], NT_DIMS) * (1.0 / total))
    sum_first.start()

    def second_1():
        near_second.wait(0, 1)
        far_second.wait(0)
        far_second.start(1)

    def second_2():
        near_second.wait(4)
        near_second.start(7)
        near_second.wait(3)
        near_second.start(9, 11)
        near_second.wait(6)
        near_second.start(12)

    def second_3():
        sum_first.ring(0)
        far_second.wait(1)
        far_second.start(2)

    def second_4():
        near_second.wait(7)
        near_second.start(13)
        near_second.wait(8, 9, 10, 11)

    def second_5():
        near_second.wait(12, 13)
        sum_first.ring(1)

    def second_7():
        far_second.turn()
        sum_first.ring(2)

    run(
        0, 8, False, vectors2,
        {1: second_1, 2: second_2, 3: second_3, 4: second_4, 5: second_5, 7: second_7},
    )
    far_second.wait_other()
    finish_row(coeffs2, 2 * R, 0)
    finish_row(coeffs2, 2 * R, 1)

    newest = field[2 * R :, :]
    cross = close(newest, field[0 : 2 * R, :], NT_DIMS) * (1.0 / total)
    part2[...] = pack(cross, close(newest, newest, NT_DIMS) * (1.0 / total))
    sum_second.start()
    sum_first.wait()
    gram, first_gram = unpack(full[...])
    inverse0, upper0 = cholesky(first_gram)
    small_ref[0] = upper0
    small_ref[3] = inverse0
    sum_second.ring(0)
    both = exact(inverse0, gram)
    cross = exact(both[:, :R], inverse0, NT_DIMS)
    square = exact(pltpu.roll(both, R, 1)[:, :R], inverse0, NT_DIMS) - exact(cross, cross, NT_DIMS)
    small_ref[1] = cross
    left[0:R, :] = close(inverse0, field[0:R, :])
    sum_second.ring(1)
    inverse1, upper1 = cholesky(jnp.concatenate([square, jnp.zeros((R, R), F32)], axis=1))
    small_ref[2] = upper1
    mix = jnp.concatenate([-exact(exact(inverse1, cross), inverse0), exact(inverse1, inverse0)], axis=1)
    mixes_ref[0] = gram
    mixes_ref[1] = mix
    sum_second.ring(2)
    left[R : 2 * R, :] = close(mix, field[0 : 2 * R, :])
    early = pltpu.make_async_copy(left.at[pl.ds(0, 2 * R)], left_ref.at[pl.ds(0, 2 * R)], left_sem.at[0])
    early.start()
    left[2 * R :, :] = close(mix, field[R:, :])
    late = pltpu.make_async_copy(left.at[pl.ds(2 * R, R)], left_ref.at[pl.ds(2 * R, R)], left_sem.at[1])
    late.start()
    for gather in (near_space, near_first, near_second, far_first, far_second, sum_first):
        gather.finish()
    early.wait()
    late.wait()
    sum_second.wait()
    sums_ref[...] = full2[...]
    sum_second.finish()


def last_kernel(left_hbm, sums_ref, small_ref, mixes_ref, one_ref, two_ref, factors_ref, left_ref, sem):
    fetch = pltpu.make_async_copy(left_hbm, left_ref, sem.at[0])
    fetch.start()
    hand_on = pltpu.make_async_copy(left_ref.at[pl.ds(R, R)], one_ref, sem.at[1])
    inverse0 = small_ref[3]
    gram, mix = mixes_ref[0], mixes_ref[1]
    cross, square = unpack(sums_ref[...])
    pair = exact(mix, jnp.concatenate([gram, cross], axis=0))
    heads0 = exact(pair[:, :R], inverse0, NT_DIMS)
    heads1 = exact(pair, mix, NT_DIMS)
    cross = pltpu.roll(cross, R, 1)[:, :R]
    square = jnp.concatenate(
        [
            jnp.concatenate([pltpu.roll(gram, R, 1)[:, :R], cross.T], axis=1),
            jnp.concatenate([cross, square[:, :R]], axis=1),
        ],
        axis=0,
    )
    rest = exact(exact(mix, square), mix, NT_DIMS) - exact(heads0, heads0, NT_DIMS) - exact(heads1, heads1, NT_DIMS)
    fetch.wait()
    hand_on.start()
    inverse, upper = cholesky(jnp.concatenate([rest, jnp.zeros((R, R), F32)], axis=1))
    last = jnp.concatenate([-close(inverse, heads0), -close(inverse, heads1)], axis=1)
    two_ref[...] = close(last, left_ref[: 2 * R, :]) + close(inverse, left_ref[2 * R :, :])
    row = lax.broadcasted_iota(jnp.int32, (R, R), 0)
    lane = lax.broadcasted_iota(jnp.int32, (R, R), 1)
    half = jnp.where(row == lane, 0.5, 0.0)
    factors_ref[0] = small_ref[0].T
    factors_ref[1] = small_ref[1].T + half
    factors_ref[2] = small_ref[2].T
    factors_ref[3] = heads0.T
    factors_ref[4] = heads1.T + half
    factors_ref[5] = upper.T
    hand_on.wait()


def on_device(residual, panels, near_list, near_len, far_list, basis_far, coupling):
    vmem = pl.BlockSpec(memory_space=pltpu.VMEM)
    smem = pl.BlockSpec(memory_space=pltpu.SMEM)
    hbm = pl.BlockSpec(memory_space=pl.ANY)
    wide = jax.ShapeDtypeStruct((R, 2 * B), F32)
    sums = [
        pltpu.VMEM((8, 16, 2 * R), F32),
        pltpu.VMEM((8, 16, 2 * R), F32),
        pltpu.VMEM((2, 4, 16, 2 * R), F32),
        pltpu.VMEM((8, 16, 2 * R), F32),
    ]
    left, sums_all, small, mixes, _ = pl.pallas_call(
        step_kernel,
        out_shape=(
            jax.ShapeDtypeStruct((3 * R, 2 * B), F32),
            jax.ShapeDtypeStruct((8, 16, 2 * R), F32),
            jax.ShapeDtypeStruct((4, R, R), F32),
            jax.ShapeDtypeStruct((2, R, 2 * R), F32),
            jax.ShapeDtypeStruct((PAIRS, 2, B, B), BF16),
        ),
        in_specs=[hbm, hbm, vmem, smem, smem, vmem, hbm, hbm],
        out_specs=(pl.BlockSpec(memory_space=pl.ANY), vmem, vmem, vmem, pl.BlockSpec(memory_space=pl.ANY)),
        scratch_shapes=[
            pltpu.VMEM((3 * R, 2 * B), F32),
            pltpu.VMEM((8, 2, DEPTH, B), BF16),
            pltpu.VMEM((8, 2, R, B), BF16),
            pltpu.VMEM((8, 2, R, B), BF16),
            pltpu.VMEM((2, 128, K // 2, 2 * R), BF16),
            pltpu.VMEM((2, 128, K // 2, 2 * R), BF16),
            pltpu.VMEM((PAIRS + 2, 2, B, B), BF16),
            pltpu.VMEM((2, R, B), F32),
            pltpu.VMEM((2, 16, 128), F32),
            pltpu.VMEM((2, DEPTH, B), F32),
            pltpu.VMEM((2, DEPTH, B), BF16),
            pltpu.VMEM((2, 4 * K, NF * K), BF16),
            pltpu.VMEM((NF * K, 2 * R), BF16),
            *sums,
            *sums,
            pltpu.VMEM((3 * R, 2 * B), F32),
            pltpu.SemaphoreType.DMA((3, 14)),
            pltpu.SemaphoreType.DMA((3, 14)),
            pltpu.SemaphoreType.DMA((2, 26)),
            pltpu.SemaphoreType.DMA((2, 26)),
            pltpu.SemaphoreType.DMA((2, 20)),
            pltpu.SemaphoreType.DMA((2, 20)),
            pltpu.SemaphoreType.DMA((2,)),
            pltpu.SemaphoreType.DMA((2,)),
            pltpu.SemaphoreType.DMA((2,)),
            pltpu.VMEM((R, 2 * B), F32),
            pltpu.VMEM((2, 4, B), F32),
            pltpu.VMEM((2, K, B), F32),
            pltpu.VMEM((2, K, NF * K), F32),
            pltpu.SemaphoreType.DMA((4,)),
        ],
        compiler_params=pltpu.CompilerParams(
            collective_id=0, has_side_effects=True, vmem_limit_bytes=62 * 2**20
        ),
        cost_estimate=pl.CostEstimate(flops=17_000_000_000, bytes_accessed=80_000_000, transcendentals=33_554_432),
    )(residual.T, panels, near_list, near_len, far_list, far_list, basis_far, coupling)
    one, two, factors = pl.pallas_call(
        last_kernel,
        out_shape=(wide, wide, jax.ShapeDtypeStruct((6, R, R), F32)),
        in_specs=[pl.BlockSpec(memory_space=pl.ANY), vmem, vmem, vmem],
        out_specs=(pl.BlockSpec(memory_space=pl.ANY), vmem, vmem),
        scratch_shapes=[pltpu.VMEM((3 * R, 2 * B), F32), pltpu.SemaphoreType.DMA((2,))],
        cost_estimate=pl.CostEstimate(flops=150_000_000, bytes_accessed=3_000_000, transcendentals=64),
    )(left, sums_all, small, mixes)
    return (one.T, two.T, factors)


def solution(mesh):
    return jax.shard_map(
        on_device,
        mesh=mesh,
        in_specs=(
            P(("wide", "group"), None),
            P(("wide", "group"), None, None),
            P(("wide", "group"), None),
            P(("wide", "group")),
            P(("wide", "group"), None),
            P(("wide", "group"), None, None),
            P(("wide", "group"), None, None),
        ),
        out_specs=(P(("wide", "group"), None), P(("wide", "group"), None), P()),
        check_vma=False,
    )
```
